256 devices in a mesh: seq: 8 (over z_hi, core), chan: 32 (over y, x, z_lo).
Axes of the slice: x: 4, y: 4, z: 8 (z_hi: 4, z_lo: 2; z = z_hi * 2 + z_lo), core: 2. Of those that a mesh axis runs over, the one named last changes fastest.
Arguments:
- signal: bfloat16 [4096, 4096], P('seq', 'chan'), may hold values from -6 to 6
- gating: bfloat16 [4096, 4096], P('seq', 'chan'), may hold values from -6 to 6
- filter_taps: bfloat16 [4096, 4096], P('seq', 'chan'), may hold values from -0.25 to 0.25
- skip_bias: float32 [4096], P('chan'), may hold values from -1 to 1
- out_weight: bfloat16 [4096, 4096], P(None, 'chan'), may hold values from -0.09375 to 0.09375
- test_matrix: bfloat16 [4096, 256], P('chan'), may hold values from -0.09375 to 0.09375
Outputs:
- mixed: bfloat16 [4096, 4096], P('seq', 'chan')
- sketch_y: float32 [4096, 256], P('seq')
- sketch_z: float32 [4096, 256], P('chan')
The draws below stay inside these ranges and needn't reach their ends.
All inputs are finite; a program needn't handle non-finite values.
Results may differ from the reference program's by a relative error of at most 0.015.
Values may be sent and summed in bfloat16 or wider, within the bound.
A program may use at most 64 MiB of HBM per device.

```python
import jax
import jax.numpy as jnp
from jax import lax

D = 4096
R = 256
SEQ = 4096


def steps_of(own_key, extent, shards, least, top_value):
    factor_of = 1.0
    for axis_at, blocks in shards:
        heights = jax.random.uniform(jax.random.fold_in(jax.random.fold_in(own_key, 6), axis_at), (blocks,), jnp.float32, least / len(shards), top_value / len(shards))
        factor_of = factor_of * jnp.repeat(jnp.exp(heights), extent[axis_at] // blocks).reshape((-1,) + (1,) * (len(extent) - 1 - axis_at))
    return factor_of


def gaussian(rng, shape, deviation, bound, split=(), dtype=jnp.bfloat16):
    loudness = steps_of(rng, shape, split, -0.22, 0.18) if split else 1.0
    array = jax.random.normal(rng, shape, jnp.float32) * deviation * loudness
    return jnp.minimum(jnp.maximum(array, -bound), bound).astype(dtype)


def setup_inputs(seed: int = 0) -> dict:
    key_list = jax.random.split(jax.random.key(seed), 7)
    return {
        "signal": gaussian(key_list[0], (SEQ, D), 1.0, 6.0, ((0, 8), (1, 32))),
        "gating": gaussian(key_list[1], (SEQ, D), 1.0, 6.0, ((0, 8), (1, 32))),
        "filter_taps": gaussian(key_list[2], (SEQ, D), (SEQ ** -0.5), 0.25, ((0, 8), (1, 32))),
        "skip_bias": jnp.clip(jax.random.uniform(key_list[3], (D,), jnp.float32, -1.0, 1.0) * steps_of(key_list[3], (D,), ((0, 32),), -0.4, 0.0), -1.0, 1.0),
        "out_weight": gaussian(key_list[4], (D, D), D ** -0.5, 0.09375, ((1, 32),)),
        "test_matrix": gaussian(key_list[5], (D, R), (D ** -0.5), 0.09375, ((0, 32),)),
    }


def reference(signal, gating, filter_taps, skip_bias, out_weight, test_matrix):
    values = signal.astype(jnp.float32)
    taps = filter_taps.astype(jnp.float32)
    fft_len = 2 * SEQ
    spectrum = jnp.fft.rfft(values, n=fft_len, axis=0) * jnp.fft.rfft(taps, n=fft_len, axis=0)
    convolved = jnp.fft.irfft(spectrum, n=fft_len, axis=0)[:SEQ].astype(jnp.float32)
    gated = (gating.astype(jnp.float32) * (convolved + skip_bias[None, :] * values)).astype(jnp.bfloat16)
    projected = jnp.dot(gated, out_weight, preferred_element_type=jnp.float32)
    mixed = projected.astype(jnp.bfloat16)
    sketch_y = jnp.dot(projected, test_matrix.astype(jnp.float32), precision=lax.Precision.HIGHEST)
    sketch_z = jnp.dot(projected.T, sketch_y, precision=lax.Precision.HIGHEST) / SEQ
    return mixed, sketch_y, sketch_z
```

```python
import functools
import math

import jax
import jax.numpy as jnp
import numpy as np
from jax import lax
from jax.experimental import pallas as pl
from jax.experimental.pallas import tpu as pltpu
from jax.sharding import PartitionSpec as P

MESH = pl.DeviceIdType.MESH
F32, BF16 = jnp.float32, jnp.bfloat16

SEQ_DEV = 8
CHAN_DEV = 32
NEAR = 8
FAR = 4
ROWS = 512
CHANS = 128
SUB = 64
LANES = 16
COARSE = 9
RANK = 256


def split_np(x):
    high = x.astype(jnp.bfloat16)
    low = (x - high.astype(np.float64)).astype(jnp.bfloat16)
    return high, low


@functools.lru_cache(None)
def tables():
    n = 2 * SEQ_DEV * ROWS
    j = np.arange(SUB)
    q = np.arange(8)
    b = np.arange(8)
    turn = []
    fwd, inv = [], []
    eye = np.eye(LANES)
    for a in range(COARSE):
        k1 = a + 16 * b
        angle = 2 * np.pi * np.outer(j, k1) / n
        turn.append((np.repeat(np.cos(angle), LANES, 1), np.repeat(np.sin(angle), LANES, 1)))
        ang = 2 * np.pi * np.outer(q, k1) / 128
        c, s = np.kron(np.cos(ang), eye), np.kron(np.sin(ang), eye)
        fwd.append(np.block([[c, -s], [s, c]]))
        weight = (1.0 if a in (0, 8) else 2.0) / n
        inv.append(np.block([[c.T, s.T], [-s.T, c.T]]) * weight)
    fine = 2 * np.pi * np.outer(j, j) / SUB
    c, s = np.cos(fine), np.sin(fine)
    left = np.block([[c, s], [-s, c]])
    left_inv = np.block([[c, -s], [s, c]])

    def triple(m):
        high, low = split_np(m)
        return np.concatenate([high, high, low], 1)

    fwd_hi, fwd_lo = split_np(np.stack(fwd))
    inv_hi, inv_lo = split_np(np.stack(inv))
    turn = np.stack([np.stack(t) for t in turn]).astype(np.float32)
    return turn, np.stack([triple(left), triple(left_inv)]), fwd_hi, fwd_lo, inv_hi, inv_lo


def dot(a, b):
    return lax.dot_general(a, b, (((1,), (0,)), ((), ())), preferred_element_type=F32)


def split(x):
    high = x.astype(BF16)
    return high, (x - high.astype(F32)).astype(BF16)


def block_transpose(blocks):
    lane = lax.broadcasted_iota(jnp.int32, (SUB, 128), 1)
    for bit in range(3):
        step = LANES << bit
        low = (lane & step) == 0
        new = list(blocks)
        for q in range(8):
            if q >> bit & 1:
                continue
            p = q | 1 << bit
            new[q] = jnp.where(low, blocks[q], pltpu.roll(blocks[p], step, 1))
            new[p] = jnp.where(low, pltpu.roll(blocks[q], 128 - step, 1), blocks[p])
        blocks = new
    return blocks


def coarse_forward(x):
    plus = {s: x[s] + x[8 - s] for s in (1, 2, 3)}
    minus = {s: x[s] - x[8 - s] for s in (1, 2, 3)}

    def total(terms):
        out = None
        for factor, value in terms:
            if abs(factor) < 1e-9:
                continue
            if abs(factor - 1) < 1e-9:
                term = value
            elif abs(factor + 1) < 1e-9:
                term = -value
            else:
                term = value * np.float32(factor)
            out = term if out is None else out + term
        return jnp.zeros_like(x[0]) if out is None else out

    result = []
    for a in range(COARSE):
        cos = lambda s: math.cos(2 * math.pi * s * a / 16)
        sin = lambda s: math.sin(2 * math.pi * s * a / 16)
        even, odd = (plus, minus) if a % 2 == 0 else (minus, plus)
        re = total([(1.0, x[0]), (cos(4), x[4])] + [(cos(s), even[s]) for s in (1, 2, 3)])
        im = total([(-sin(4), x[4])] + [(-sin(s), odd[s]) for s in (1, 2, 3)])
        result.append((re, im))
    return result


def kernel(
    sig, gat, fil, skip, w, test, turn, left, fwd_hi, fwd_lo, inv_hi, inv_lo,
    mixed, out_y, out_z,
    send_a, recv_a, send_b, recv_b, depth, w_group, part, recv_p,
    send_y, recv_y, full_y, send_z, recv_z, full_z, spec, back,
    sem_a, sem_b, sem_g, sem_w, sem_p, sem_y, sem_v, sem_z, sem_t, sem_w0,
):
    me_s, me_c = lax.axis_index("seq"), lax.axis_index("chan")
    group, near = me_c // NEAR, me_c % NEAR

    def on_seq(k):
        return {"seq": lax.rem(me_s + k, SEQ_DEV), "chan": me_c}

    def on_chan(k):
        return {"seq": me_s, "chan": lax.rem(me_c + k, CHAN_DEV)}

    def on_near(k):
        return {"seq": me_s, "chan": group * NEAR + lax.rem(near + k, NEAR)}

    def on_far(k):
        return {"seq": me_s, "chan": lax.rem(me_c + NEAR * k, CHAN_DEV)}

    def remote(src, dst, sems, k, target):
        copy = pltpu.make_async_remote_copy(
            src_ref=src, dst_ref=dst, send_sem=sems.at[0, k], recv_sem=sems.at[1, k],
            device_id=target, device_id_type=MESH,
        )
        copy.start()
        return copy

    barrier = pltpu.get_barrier_semaphore()
    for k in range(1, SEQ_DEV):
        pl.semaphore_signal(barrier, inc=1, device_id=on_seq(k), device_id_type=MESH)
    for k in range(1, CHAN_DEV):
        pl.semaphore_signal(barrier, inc=1, device_id=on_chan(k), device_id_type=MESH)

    for at, source in enumerate((sig, fil)):
        blocks = [source[q * SUB : (q + 1) * SUB, :].astype(F32) for q in range(8)]
        for d, block in enumerate(block_transpose(blocks)):
            send_a[d, at * SUB : (at + 1) * SUB, :] = block.astype(BF16)

    pl.semaphore_wait(barrier, SEQ_DEV - 1 + CHAN_DEV - 1)

    copies_a = [
        remote(send_a.at[lax.rem(me_s + k, SEQ_DEV)], recv_a.at[me_s], sem_a, k, on_seq(k))
        for k in range(1, SEQ_DEV)
    ]
    recv_a[me_s] = send_a[me_s]
    columns = pl.ds(pl.multiple_of(group * CHANS, CHANS), CHANS)
    copies_w = []
    for k in range(1, FAR):
        target = lax.rem(group + k, FAR)
        rows = pl.ds(pl.multiple_of(target * NEAR * CHANS, NEAR * CHANS), NEAR * CHANS)
        copies_w.append(remote(w.at[rows, :], w_group.at[:, columns], sem_w, k, on_far(k)))
    own_rows = pl.ds(pl.multiple_of(group * NEAR * CHANS, NEAR * CHANS), NEAR * CHANS)
    own_w = pltpu.make_async_copy(w.at[own_rows, :], w_group.at[:, columns], sem_w0)
    own_w.start()
    for copy in copies_a:
        copy.wait()

    for at in range(2):
        blocks = [recv_a[s, at * SUB : (at + 1) * SUB, :].astype(F32) for s in range(SEQ_DEV)]
        for a, (re, im) in enumerate(coarse_forward(blocks)):
            spec[a, at * SUB : (at + 1) * SUB, :128] = re
            spec[a, at * SUB : (at + 1) * SUB, 128:] = im
    for a in range(COARSE):
        high, low = split(spec[a])
        z = dot(high, fwd_hi[a]) + dot(low, fwd_hi[a]) + dot(high, fwd_lo[a])
        cos, sin = turn[a, 0], turn[a, 1]
        halves = []
        for at in range(2):
            re, im = z[at * SUB : (at + 1) * SUB, :128], z[at * SUB : (at + 1) * SUB, 128:]
            halves.append(jnp.concatenate([re * cos + im * sin, im * cos - re * sin], 0))
        high, low = split(jnp.concatenate(halves, 1))
        f = dot(left[0], jnp.concatenate([high, low, high], 0))
        sr, si, fr, fi = f[:SUB, :128], f[SUB:, :128], f[:SUB, 128:], f[SUB:, 128:]
        high, low = split(jnp.concatenate([sr * fr - si * fi, sr * fi + si * fr], 0))
        g = dot(left[1], jnp.concatenate([high, low, high], 0))
        re, im = g[:SUB], g[SUB:]
        high, low = split(jnp.concatenate([re * cos - im * sin, im * cos + re * sin], 1))
        back[a] = dot(high, inv_hi[a]) + dot(low, inv_hi[a]) + dot(high, inv_lo[a])
    for s in range(5):
        sums = {}
        for a in range(COARSE):
            cos, sin = math.cos(2 * math.pi * s * a / 16), math.sin(2 * math.pi * s * a / 16)
            for name, factor, lanes in (("c", cos, 0), ("s", sin, 128)):
                if abs(factor) > 1e-9:
                    term = back[a, :, lanes : lanes + 128] * np.float32(factor)
                    key = name + "eo"[a % 2]
                    sums[key] = sums[key] + term if key in sums else term
        zero = jnp.zeros((SUB, 128), F32)
        ce, co, se, so = (sums.get(key, zero) for key in ("ce", "co", "se", "so"))
        send_b[s] = (ce + co - se - so).astype(BF16)
        if s in (1, 2, 3):
            send_b[8 - s] = (ce - co + se - so).astype(BF16)

    copies_b = [
        remote(send_b.at[lax.rem(me_s + k, SEQ_DEV)], recv_b.at[me_s], sem_b, k, on_seq(k))
        for k in range(1, SEQ_DEV)
    ]
    recv_b[me_s] = send_b[me_s]
    for copy in copies_b:
        copy.wait()
    near_columns = pl.ds(pl.multiple_of(near * CHANS, CHANS), CHANS)
    convolved = block_transpose([recv_b[d].astype(F32) for d in range(8)])
    for q in range(8):
        rows = slice(q * SUB, (q + 1) * SUB)
        value = convolved[q] + skip[...] * sig[rows, :].astype(F32)
        depth[rows, near_columns] = (gat[rows, :].astype(F32) * value).astype(BF16)

    copies_g = [
        remote(depth.at[:, near_columns], depth.at[:, near_columns], sem_g, k, on_near(k))
        for k in range(1, NEAR)
    ]
    own_w.wait()
    for copy in copies_w:
        copy.wait()
    for copy in copies_g:
        copy.wait()

    for f in range(FAR):
        lanes = slice(f * CHANS, (f + 1) * CHANS)
        part[f] = dot(depth[...], w_group[:, lanes]).astype(BF16)
    copies_p = [
        remote(part.at[lax.rem(group + k, FAR)], recv_p.at[group], sem_p, k, on_far(k))
        for k in range(1, FAR)
    ]
    recv_p[group] = part[group]
    for copy in copies_p:
        copy.wait()
    projected = recv_p[0].astype(F32)
    for f in range(1, FAR):
        projected = projected + recv_p[f].astype(F32)
    high, low = split(projected)
    mixed[...] = high
    partial_y = dot(high, test[...]) + dot(low, test[...])
    for c in range(CHAN_DEV):
        send_y[c] = partial_y[c * 16 : (c + 1) * 16, :].astype(BF16)
    copies_y = [
        remote(send_y.at[lax.rem(me_c + k, CHAN_DEV)], recv_y.at[me_c], sem_y, k, on_chan(k))
        for k in range(1, CHAN_DEV)
    ]
    recv_y[me_c] = send_y[me_c]
    for copy in copies_y:
        copy.wait()
    total = recv_y[0].astype(F32)
    for c in range(1, CHAN_DEV):
        total = total + recv_y[c].astype(F32)
    full_y[me_c] = total.astype(BF16)
    copies_v = [
        remote(full_y.at[me_c], full_y.at[me_c], sem_v, k, on_chan(k)) for k in range(1, CHAN_DEV)
    ]
    for copy in copies_v:
        copy.wait()
    sketch = full_y[...].reshape(ROWS, RANK)
    out_y[...] = sketch.astype(F32)
    partial_z = lax.dot_general(
        high, sketch, (((0,), (0,)), ((), ())), preferred_element_type=F32
    ) * np.float32(1.0 / (SEQ_DEV * ROWS))
    for s in range(SEQ_DEV):
        send_z[s] = partial_z[s * 16 : (s + 1) * 16, :].astype(BF16)
    copies_z = [
        remote(send_z.at[lax.rem(me_s + k, SEQ_DEV)], recv_z.at[me_s], sem_z, k, on_seq(k))
        for k in range(1, SEQ_DEV)
    ]
    recv_z[me_s] = send_z[me_s]
    for copy in copies_z:
        copy.wait()
    total = recv_z[0].astype(F32)
    for s in range(1, SEQ_DEV):
        total = total + recv_z[s].astype(F32)
    full_z[me_s] = total.astype(BF16)
    copies_t = [
        remote(full_z.at[me_s], full_z.at[me_s], sem_t, k, on_seq(k)) for k in range(1, SEQ_DEV)
    ]
    for copy in copies_t:
        copy.wait()
    out_z[...] = full_z[...].reshape(CHANS, RANK).astype(F32)


def per_device(signal, gating, filter_taps, skip_bias, out_weight, test_matrix):
    vmem = pl.BlockSpec(memory_space=pltpu.VMEM)
    constants = [jnp.asarray(t) for t in tables()]
    args = [signal, gating, filter_taps, skip_bias[None, :], out_weight, test_matrix] + constants

    def sems(n):
        return pltpu.SemaphoreType.DMA((2, n))

    return pl.pallas_call(
        kernel,
        out_shape=(
            jax.ShapeDtypeStruct((ROWS, CHANS), BF16),
            jax.ShapeDtypeStruct((ROWS, RANK), F32),
            jax.ShapeDtypeStruct((CHANS, RANK), F32),
        ),
        in_specs=[vmem] * len(args),
        out_specs=(vmem, vmem, vmem),
        scratch_shapes=[
            pltpu.VMEM((SEQ_DEV, 2 * SUB, 128), BF16),
            pltpu.VMEM((SEQ_DEV, 2 * SUB, 128), BF16),
            pltpu.VMEM((SEQ_DEV, SUB, 128), BF16),
            pltpu.VMEM((SEQ_DEV, SUB, 128), BF16),
            pltpu.VMEM((ROWS, NEAR * CHANS), BF16),
            pltpu.VMEM((NEAR * CHANS, FAR * CHANS), BF16),
            pltpu.VMEM((FAR, ROWS, CHANS), BF16),
            pltpu.VMEM((FAR, ROWS, CHANS), BF16),
            pltpu.VMEM((CHAN_DEV, 16, RANK), BF16),
            pltpu.VMEM((CHAN_DEV, 16, RANK), BF16),
            pltpu.VMEM((CHAN_DEV, 16, RANK), BF16),
            pltpu.VMEM((SEQ_DEV, 16, RANK), BF16),
            pltpu.VMEM((SEQ_DEV, 16, RANK), BF16),
            pltpu.VMEM((SEQ_DEV, 16, RANK), BF16),
            pltpu.VMEM((COARSE, 2 * SUB, 256), F32),
            pltpu.VMEM((COARSE, SUB, 256), F32),
            sems(SEQ_DEV), sems(SEQ_DEV), sems(NEAR), sems(FAR), sems(FAR),
            sems(CHAN_DEV), sems(CHAN_DEV), sems(SEQ_DEV), sems(SEQ_DEV),
            pltpu.SemaphoreType.DMA,
        ],
        compiler_params=pltpu.CompilerParams(
            collective_id=0, has_side_effects=True, vmem_limit_bytes=48 * 2**20
        ),
    )(*args)


def solution(mesh):
    return jax.shard_map(
        per_device,
        mesh=mesh,
        in_specs=(
            P("seq", "chan"), P("seq", "chan"), P("seq", "chan"),
            P("chan"), P(None, "chan"), P("chan", None),
        ),
        out_specs=(P("seq", "chan"), P("seq", None), P("chan", None)),
        check_vma=False,
    )
```

```python
import functools
import math

import jax
import jax.numpy as jnp
import numpy as np
from jax import lax
from jax.experimental import pallas as pl
from jax.experimental.pallas import tpu as pltpu
from jax.sharding import PartitionSpec as P

MESH = pl.DeviceIdType.MESH
F32, BF16 = jnp.float32, jnp.bfloat16

SEQ_DEV = 8
CHAN_DEV = 32
NEAR = 8
FAR = 4
ROWS = 512
CHANS = 128
SUB = 64
LANES = 16
COARSE = 9
RANK = 256
SLICE = RANK // NEAR
CHUNKS = 4
STEP = ROWS // CHUNKS
HALF = ROWS // 2
SEQ_ORDER = (4, 3, 5, 2, 6, 1, 7)


def split_np(x):
    high = x.astype(jnp.bfloat16)
    low = (x - high.astype(np.float64)).astype(jnp.bfloat16)
    return high, low


@functools.lru_cache(None)
def tables():
    n = 2 * SEQ_DEV * ROWS
    j = np.arange(SUB)
    q = np.arange(8)
    b = np.arange(8)
    turn = []
    fwd, inv = [], []
    eye = np.eye(LANES)
    for a in range(COARSE):
        k1 = a + 16 * b
        angle = 2 * np.pi * np.outer(j, k1) / n
        turn.append((np.repeat(np.cos(angle), LANES, 1), np.repeat(np.sin(angle), LANES, 1)))
        ang = 2 * np.pi * np.outer(q, k1) / 128
        c, s = np.kron(np.cos(ang), eye), np.kron(np.sin(ang), eye)
        fwd.append(np.block([[c, -s], [s, c]]))
        weight = (1.0 if a in (0, 8) else 2.0) / n
        inv.append(np.block([[c.T, s.T], [-s.T, c.T]]) * weight)
    fine = 2 * np.pi * np.outer(j, j) / SUB
    c, s = np.cos(fine), np.sin(fine)
    left = np.block([[c, s], [-s, c]])
    left_inv = np.block([[c, -s], [s, c]])

    def triple(m):
        high, low = split_np(m)
        return np.concatenate([high, high, low], 1)

    fwd = np.stack(split_np(np.stack(fwd)))
    inv = np.stack(split_np(np.stack(inv)))
    turn = np.stack([np.stack(t) for t in turn]).astype(np.float32)
    return turn, np.stack([triple(left), triple(left_inv)]), fwd, inv


def dot(a, b):
    return lax.dot_general(a, b, (((1,), (0,)), ((), ())), preferred_element_type=F32)


def split(x):
    high = x.astype(BF16)
    return high, (x - high.astype(F32)).astype(BF16)


def block_transpose(blocks):
    lane = lax.broadcasted_iota(jnp.int32, (SUB, 128), 1)
    for bit in range(3):
        step = LANES << bit
        low = (lane & step) == 0
        new = list(blocks)
        for q in range(8):
            if q >> bit & 1:
                continue
            p = q | 1 << bit
            new[q] = jnp.where(low, blocks[q], pltpu.roll(blocks[p], step, 1))
            new[p] = jnp.where(low, pltpu.roll(blocks[q], 128 - step, 1), blocks[p])
        blocks = new
    return blocks


def coarse_forward(x):
    plus = {s: x[s] + x[8 - s] for s in (1, 2, 3)}
    minus = {s: x[s] - x[8 - s] for s in (1, 2, 3)}

    def total(terms):
        out = None
        for factor, value in terms:
            if abs(factor) < 1e-9:
                continue
            if abs(factor - 1) < 1e-9:
                term = value
            elif abs(factor + 1) < 1e-9:
                term = -value
            else:
                term = value * np.float32(factor)
            out = term if out is None else out + term
        return jnp.zeros_like(x[0]) if out is None else out

    result = []
    for a in range(COARSE):
        cos = lambda s: math.cos(2 * math.pi * s * a / 16)
        sin = lambda s: math.sin(2 * math.pi * s * a / 16)
        even, odd = (plus, minus) if a % 2 == 0 else (minus, plus)
        re = total([(1.0, x[0]), (cos(4), x[4])] + [(cos(s), even[s]) for s in (1, 2, 3)])
        im = total([(-sin(4), x[4])] + [(-sin(s), odd[s]) for s in (1, 2, 3)])
        result.append((re, im))
    return result


def kernel(
    sig_in, gat_in, fil_in, skip_in, w, test_in, turn_in, left_in, fwd_in, inv_in,
    mixed, out_y, out_z,
    sig, gat, fil, skip, turn, left, fwd, inv, sem_in,
    send_a, recv_a, send_b, recv_b, depth, w_group, part, recv_p, spec, back,
    test, w_rows, send_v, recv_v, v_own, v_near, send_y, recv_y, full_y,
    part_z, send_z, recv_z, recv_h, full_z,
    sem_a, sem_b, sem_g, sem_w, sem_r, sem_e, sem_v, sem_u, sem_p, sem_q, sem_y, sem_c, sem_h, sem_f,
):
    me_s, me_c = lax.axis_index("seq"), lax.axis_index("chan")
    group, near, core = me_c // NEAR, me_c % NEAR, me_s % 2

    def on_seq(k):
        return {"seq": lax.rem(me_s + k, SEQ_DEV), "chan": me_c}

    def on_chan(k):
        return {"seq": me_s, "chan": lax.rem(me_c + k, CHAN_DEV)}

    def on_near(k):
        return {"seq": me_s, "chan": group * NEAR + lax.rem(near + k, NEAR)}

    def on_far(k):
        return {"seq": me_s, "chan": lax.rem(me_c + NEAR * k, CHAN_DEV)}

    other_core = {"seq": me_s + 1 - 2 * core, "chan": me_c}

    def remote(src, dst, sems, k, target):
        copy = pltpu.make_async_remote_copy(
            src_ref=src, dst_ref=dst, send_sem=sems.at[0, k], recv_sem=sems.at[1, k],
            device_id=target, device_id_type=MESH,
        )
        copy.start()
        return copy

    def local(k, src, dst):
        copy = pltpu.make_async_copy(src, dst, sem_in.at[k])
        copy.start()
        return copy

    def finish(*groups):
        for copies in groups:
            for copy in copies:
                copy.wait()

    in_sig = [local(0, sig_in, sig), local(1, fil_in, fil)]
    in_tables = [
        local(2, fwd_in, fwd), local(3, turn_in, turn), local(4, left_in, left), local(5, inv_in, inv)
    ]
    in_gate = [local(6, gat_in, gat), local(7, skip_in, skip)]

    barrier = pltpu.get_barrier_semaphore()
    for k in range(1, SEQ_DEV):
        pl.semaphore_signal(barrier, inc=1, device_id=on_seq(k), device_id_type=MESH)
    for k in range(1, CHAN_DEV):
        pl.semaphore_signal(barrier, inc=1, device_id=on_chan(k), device_id_type=MESH)

    finish(in_sig)
    for at, source in enumerate((sig, fil)):
        blocks = [source[q * SUB : (q + 1) * SUB, :].astype(F32) for q in range(8)]
        for d, block in enumerate(block_transpose(blocks)):
            send_a[d, at * SUB : (at + 1) * SUB, :] = block.astype(BF16)

    pl.semaphore_wait(barrier, SEQ_DEV - 1 + CHAN_DEV - 1)

    copies_a = [
        remote(send_a.at[lax.rem(me_s + k, SEQ_DEV)], recv_a.at[me_s], sem_a, k, on_seq(k))
        for k in SEQ_ORDER
    ]

    columns = pl.ds(pl.multiple_of(group * CHANS, CHANS), CHANS)
    copies_e, copies_r, copies_w = [], [], []

    def weight_rows(target, first, count):
        return pl.ds(pl.multiple_of(target * NEAR * CHANS + first, CHANS), count)

    for k in range(1, FAR):
        rows = weight_rows(lax.rem(group + k, FAR), me_s * CHANS, CHANS)
        copies_r.append(remote(w.at[rows, :], w_rows.at[:, columns], sem_r, k, on_far(k)))
        copies_e.append(remote(test_in, test.at[group], sem_e, k, on_far(k)))
    copies_r.append(local(8, w.at[weight_rows(group, me_s * CHANS, CHANS), :], w_rows.at[:, columns]))
    copies_e.append(local(9, test_in, test.at[group]))
    for k in range(1, FAR):
        rows = weight_rows(lax.rem(group + k, FAR), 0, NEAR * CHANS)
        copies_w.append(remote(w.at[rows, :], w_group.at[:, columns], sem_w, k, on_far(k)))
    copies_w.append(local(10, w.at[weight_rows(group, 0, NEAR * CHANS), :], w_group.at[:, columns]))
    recv_a[me_s] = send_a[me_s]

    finish(copies_r, copies_e)
    product = jnp.zeros((CHANS, RANK), F32)
    for f in range(FAR):
        product = product + dot(w_rows[:, f * CHANS : (f + 1) * CHANS], test[f])
    send_v[...] = product.T.reshape(NEAR, SLICE, CHANS)
    copies_v = [
        remote(send_v.at[lax.rem(near + k, NEAR)], recv_v.at[near], sem_v, k, on_near(k))
        for k in range(1, NEAR)
    ]
    recv_v[near] = send_v[near]

    finish(in_tables, copies_a)
    for at in range(2):
        blocks = [recv_a[s, at * SUB : (at + 1) * SUB, :].astype(F32) for s in range(SEQ_DEV)]
        for a, (re, im) in enumerate(coarse_forward(blocks)):
            spec[a, at * SUB : (at + 1) * SUB, :128] = re
            spec[a, at * SUB : (at + 1) * SUB, 128:] = im
    for a in range(COARSE):
        if a == COARSE // 2:
            finish(copies_v)
            total = recv_v[0]
            for n in range(1, NEAR):
                total = total + recv_v[n]
            v_own[...] = total.astype(BF16)
            v_lanes = pl.ds(pl.multiple_of(me_s * CHANS, CHANS), CHANS)
            copies_u = [
                remote(v_own, v_near.at[:, v_lanes], sem_u, k, on_seq(k)) for k in SEQ_ORDER
            ]
            v_near[:, v_lanes] = v_own[...]
        high, low = split(spec[a])
        z = dot(high, fwd[0, a]) + dot(low, fwd[0, a]) + dot(high, fwd[1, a])
        cos, sin = turn[a, 0], turn[a, 1]
        halves = []
        for at in range(2):
            re, im = z[at * SUB : (at + 1) * SUB, :128], z[at * SUB : (at + 1) * SUB, 128:]
            halves.append(jnp.concatenate([re * cos + im * sin, im * cos - re * sin], 0))
        high, low = split(jnp.concatenate(halves, 1))
        f = dot(left[0], jnp.concatenate([high, low, high], 0))
        sr, si, fr, fi = f[:SUB, :128], f[SUB:, :128], f[:SUB, 128:], f[SUB:, 128:]
        high, low = split(jnp.concatenate([sr * fr - si * fi, sr * fi + si * fr], 0))
        g = dot(left[1], jnp.concatenate([high, low, high], 0))
        re, im = g[:SUB], g[SUB:]
        high, low = split(jnp.concatenate([re * cos - im * sin, im * cos + re * sin], 1))
        back[a] = dot(high, inv[0, a]) + dot(low, inv[0, a]) + dot(high, inv[1, a])
    for s in range(5):
        sums = {}
        for a in range(COARSE):
            cos, sin = math.cos(2 * math.pi * s * a / 16), math.sin(2 * math.pi * s * a / 16)
            for name, factor, lanes in (("c", cos, 0), ("s", sin, 128)):
                if abs(factor) > 1e-9:
                    term = back[a, :, lanes : lanes + 128] * np.float32(factor)
                    key = name + "eo"[a % 2]
                    sums[key] = sums[key] + term if key in sums else term
        zero = jnp.zeros((SUB, 128), F32)
        ce, co, se, so = (sums.get(key, zero) for key in ("ce", "co", "se", "so"))
        send_b[s] = (ce + co - se - so).astype(BF16)
        if s in (1, 2, 3):
            send_b[8 - s] = (ce - co + se - so).astype(BF16)

    copies_b = [
        remote(send_b.at[lax.rem(me_s + k, SEQ_DEV)], recv_b.at[me_s], sem_b, k, on_seq(k))
        for k in SEQ_ORDER
    ]
    recv_b[me_s] = send_b[me_s]
    finish(in_gate, copies_b)
    near_columns = pl.ds(pl.multiple_of(near * CHANS, CHANS), CHANS)
    convolved = block_transpose([recv_b[d].astype(F32) for d in range(8)])
    copies_g = []
    for i in range(CHUNKS):
        for q in range(i * 8 // CHUNKS, (i + 1) * 8 // CHUNKS):
            rows = slice(q * SUB, (q + 1) * SUB)
            value = convolved[q] + skip[...] * sig[rows, :].astype(F32)
            depth[rows, near_columns] = (gat[rows, :].astype(F32) * value).astype(BF16)
        block = depth.at[i * STEP : (i + 1) * STEP, near_columns]
        copies_g.append([remote(block, block, sem_g, i * NEAR + k, on_near(k)) for k in range(1, NEAR)])

    copies_p, copies_q, copies_y = [], [], []
    y_block = near * FAR + group

    def sum_y(half):
        lanes = slice(half * HALF, (half + 1) * HALF)
        finish(copies_q[half])
        total = recv_y[0, :, lanes]
        for f in range(1, FAR):
            total = total + recv_y[f, :, lanes]
        full_y[y_block, :, lanes] = total
        block = full_y.at[y_block, :, lanes]
        copies_y.append(
            [remote(block, block, sem_y, half * CHAN_DEV + k, on_chan(k)) for k in range(1, CHAN_DEV)]
        )

    finish(copies_w, copies_u)
    for i in range(CHUNKS):
        rows = slice(i * STEP, (i + 1) * STEP)
        if i == CHUNKS - 1:
            sum_y(0)
        finish(copies_g[i])
        block = depth[rows, :]
        sketch = lax.dot_general(
            v_near[...], block, (((1,), (1,)), ((), ())), preferred_element_type=F32
        )
        for f in range(FAR):
            send_y[f, :, rows] = sketch[f * 8 : (f + 1) * 8, :]
        if i % (CHUNKS // 2) == CHUNKS // 2 - 1:
            half = i // (CHUNKS // 2)
            lanes = slice(half * HALF, (half + 1) * HALF)
            copies_q.append(
                [
                    remote(
                        send_y.at[lax.rem(group + k, FAR), :, lanes], recv_y.at[group, :, lanes],
                        sem_q, half * FAR + k, on_far(k),
                    )
                    for k in range(1, FAR)
                ]
            )
            recv_y[group, :, lanes] = send_y[group, :, lanes]
        projected = dot(block, w_group[...])
        for f in range(FAR):
            part[f, rows, :] = projected[:, f * CHANS : (f + 1) * CHANS].astype(BF16)
        copies_p.append(
            [
                remote(
                    part.at[lax.rem(group + k, FAR), rows, :], recv_p.at[group, rows, :],
                    sem_p, i * FAR + k, on_far(k),
                )
                for k in range(1, FAR)
            ]
        )
        recv_p[group, rows, :] = part[group, rows, :]
    sum_y(1)
    for i in range(CHUNKS):
        rows = slice(i * STEP, (i + 1) * STEP)
        finish(copies_p[i])
        total = recv_p[0, rows, :].astype(F32)
        for f in range(1, FAR):
            total = total + recv_p[f, rows, :].astype(F32)
        mixed[rows, :] = total.astype(BF16)

    sum_z = jnp.zeros((RANK, CHANS), F32)
    for half in range(2):
        lanes = slice(half * HALF, (half + 1) * HALF)
        finish(copies_y[half])
        sketch = full_y[:, :, lanes].reshape(RANK, HALF).astype(BF16)
        sum_z = sum_z + dot(sketch, mixed[lanes, :])
    part_z[...] = (sum_z * np.float32(1.0 / (SEQ_DEV * ROWS))).reshape(2, CHANS, CHANS)
    send_z[...] = part_z[1 - core].astype(BF16)
    copies_c = [remote(send_z, recv_z, sem_c, 0, other_core)]
    finish(copies_c)
    high = me_s // 2
    recv_h[high] = (part_z[core] + recv_z[...].astype(F32)).astype(BF16)
    copies_h = [remote(recv_h.at[high], recv_h.at[high], sem_h, k, on_seq(2 * k)) for k in (2, 1, 3)]
    out_y[...] = full_y[...].reshape(RANK, ROWS).T
    finish(copies_h)
    total = recv_h[0].astype(F32)
    for h in range(1, 4):
        total = total + recv_h[h].astype(F32)
    full_z[core] = total.astype(BF16)
    copies_f = [remote(full_z.at[core], full_z.at[core], sem_f, 0, other_core)]
    finish(copies_f)
    out_z[...] = full_z[...].reshape(RANK, CHANS).astype(F32).T


def store(*refs):
    ins, outs, held, sems = refs[:3], refs[3:6], refs[6:9], refs[9]
    first = [pltpu.make_async_copy(a, b, sems.at[0, k]) for k, (a, b) in enumerate(zip(ins, held))]
    second = [pltpu.make_async_copy(a, b, sems.at[1, k]) for k, (a, b) in enumerate(zip(held, outs))]
    for copy in first:
        copy.start()
    for k in range(3):
        first[k].wait()
        second[k].start()
    for copy in second:
        copy.wait()


def per_device(signal, gating, filter_taps, skip_bias, out_weight, test_matrix):
    vmem = pl.BlockSpec(memory_space=pltpu.VMEM)
    constants = [jnp.asarray(t) for t in tables()]
    args = [signal, gating, filter_taps, skip_bias[None, :], out_weight, test_matrix] + constants
    outs = (
        jax.ShapeDtypeStruct((ROWS, CHANS), BF16),
        jax.ShapeDtypeStruct((ROWS, RANK), F32),
        jax.ShapeDtypeStruct((CHANS, RANK), F32),
    )

    def sems(n):
        return pltpu.SemaphoreType.DMA((2, n))

    results = pl.pallas_call(
        kernel,
        out_shape=outs,
        in_specs=[pl.BlockSpec(memory_space=pl.ANY)] * len(args),
        out_specs=(vmem, vmem, vmem),
        scratch_shapes=[
            pltpu.VMEM((ROWS, CHANS), BF16),
            pltpu.VMEM((ROWS, CHANS), BF16),
            pltpu.VMEM((ROWS, CHANS), BF16),
            pltpu.VMEM((1, CHANS), F32),
        ]
        + [pltpu.VMEM(c.shape, c.dtype) for c in constants]
        + [
            pltpu.SemaphoreType.DMA((11,)),
            pltpu.VMEM((SEQ_DEV, 2 * SUB, 128), BF16),
            pltpu.VMEM((SEQ_DEV, 2 * SUB, 128), BF16),
            pltpu.VMEM((SEQ_DEV, SUB, 128), BF16),
            pltpu.VMEM((SEQ_DEV, SUB, 128), BF16),
            pltpu.VMEM((ROWS, NEAR * CHANS), BF16),
            pltpu.VMEM((NEAR * CHANS, FAR * CHANS), BF16),
            pltpu.VMEM((FAR, ROWS, CHANS), BF16),
            pltpu.VMEM((FAR, ROWS, CHANS), BF16),
            pltpu.VMEM((COARSE, 2 * SUB, 256), F32),
            pltpu.VMEM((COARSE, SUB, 256), F32),
            pltpu.VMEM((FAR, CHANS, RANK), BF16),
            pltpu.VMEM((CHANS, FAR * CHANS), BF16),
            pltpu.VMEM((NEAR, SLICE, CHANS), F32),
            pltpu.VMEM((NEAR, SLICE, CHANS), F32),
            pltpu.VMEM((SLICE, CHANS), BF16),
            pltpu.VMEM((SLICE, NEAR * CHANS), BF16),
            pltpu.VMEM((FAR, 8, ROWS), F32),
            pltpu.VMEM((FAR, 8, ROWS), F32),
            pltpu.VMEM((CHAN_DEV, 8, ROWS), F32),
            pltpu.VMEM((2, CHANS, CHANS), F32),
            pltpu.VMEM((CHANS, CHANS), BF16),
            pltpu.VMEM((CHANS, CHANS), BF16),
            pltpu.VMEM((4, CHANS, CHANS), BF16),
            pltpu.VMEM((2, CHANS, CHANS), BF16),
            sems(SEQ_DEV), sems(SEQ_DEV), sems(CHUNKS * NEAR), sems(FAR), sems(FAR), sems(FAR),
            sems(NEAR), sems(SEQ_DEV), sems(CHUNKS * FAR), sems(2 * FAR), sems(2 * CHAN_DEV),
            sems(1), sems(4), sems(1),
        ],
        compiler_params=pltpu.CompilerParams(
            collective_id=0, has_side_effects=True, vmem_limit_bytes=60 * 2**20
        ),
    )(*args)
    return pl.pallas_call(
        store,
        out_shape=outs,
        in_specs=[pl.BlockSpec(memory_space=pl.ANY)] * 3,
        out_specs=(pl.BlockSpec(memory_space=pl.ANY),) * 3,
        scratch_shapes=[pltpu.VMEM(o.shape, o.dtype) for o in outs]
        + [pltpu.SemaphoreType.DMA((2, 3))],
        compiler_params=pltpu.CompilerParams(vmem_limit_bytes=60 * 2**20),
    )(*results)


def solution(mesh):
    return jax.shard_map(
        per_device,
        mesh=mesh,
        in_specs=(
            P("seq", "chan"), P("seq", "chan"), P("seq", "chan"),
            P("chan"), P(None, "chan"), P("chan", None),
        ),
        out_specs=(P("seq", "chan"), P("seq", None), P("chan", None)),
        check_vma=False,
    )
```

```python
import functools
import math

import jax
import jax.numpy as jnp
import numpy as np
from jax import lax
from jax.experimental import pallas as pl
from jax.experimental.pallas import tpu as pltpu
from jax.sharding import PartitionSpec as P

MESH = pl.DeviceIdType.MESH
F32, BF16 = jnp.float32, jnp.bfloat16

SEQ_DEV = 8
CHAN_DEV = 32
NEAR = 8
FAR = 4
ROWS = 512
CHANS = 128
SUB = 64
LANES = 16
COARSE = 9
RANK = 256
SLICE = RANK // NEAR
CHUNKS = 4
STEP = ROWS // CHUNKS
HALF = ROWS // 2
WEIGHT_HALF = NEAR * CHANS // 2
SEQ_ORDER = (4, 3, 5, 2, 6, 1, 7)


def split_np(x):
    high = x.astype(jnp.bfloat16)
    low = (x - high.astype(np.float64)).astype(jnp.bfloat16)
    return high, low


@functools.lru_cache(None)
def tables():
    n = 2 * SEQ_DEV * ROWS
    j = np.arange(SUB)
    q = np.arange(8)
    b = np.arange(8)
    turn = []
    fwd, inv = [], []
    eye = np.eye(LANES)
    for a in range(COARSE):
        k1 = a + 16 * b
        angle = 2 * np.pi * np.outer(j, k1) / n
        turn.append((np.repeat(np.cos(angle), LANES, 1), np.repeat(np.sin(angle), LANES, 1)))
        ang = 2 * np.pi * np.outer(q, k1) / 128
        c, s = np.kron(np.cos(ang), eye), np.kron(np.sin(ang), eye)
        fwd.append(np.block([[c, -s], [s, c]]))
        weight = (1.0 if a in (0, 8) else 2.0) / n
        inv.append(np.block([[c.T, s.T], [-s.T, c.T]]) * weight)
    fine = 2 * np.pi * np.outer(j, j) / SUB
    c, s = np.cos(fine), np.sin(fine)
    left = np.block([[c, s], [-s, c]])
    left_inv = np.block([[c, -s], [s, c]])

    def triple(m):
        high, low = split_np(m)
        return np.concatenate([high, high, low], 1)

    fwd = np.stack(split_np(np.stack(fwd)))
    inv = np.stack(split_np(np.stack(inv)))
    turn = np.stack([np.stack(t) for t in turn]).astype(np.float32)
    return turn, np.stack([triple(left), triple(left_inv)]), fwd, inv


def dot(a, b):
    return lax.dot_general(a, b, (((1,), (0,)), ((), ())), preferred_element_type=F32)


def split(x):
    high = x.astype(BF16)
    return high, (x - high.astype(F32)).astype(BF16)


def block_transpose(blocks):
    lane = lax.broadcasted_iota(jnp.int32, (SUB, 128), 1)
    for bit in range(3):
        step = LANES << bit
        low = (lane & step) == 0
        new = list(blocks)
        for q in range(8):
            if q >> bit & 1:
                continue
            p = q | 1 << bit
            new[q] = jnp.where(low, blocks[q], pltpu.roll(blocks[p], step, 1))
            new[p] = jnp.where(low, pltpu.roll(blocks[q], 128 - step, 1), blocks[p])
        blocks = new
    return blocks


def coarse_forward(x):
    plus = {s: x[s] + x[8 - s] for s in (1, 2, 3)}
    minus = {s: x[s] - x[8 - s] for s in (1, 2, 3)}

    def total(terms):
        out = None
        for factor, value in terms:
            if abs(factor) < 1e-9:
                continue
            if abs(factor - 1) < 1e-9:
                term = value
            elif abs(factor + 1) < 1e-9:
                term = -value
            else:
                term = value * np.float32(factor)
            out = term if out is None else out + term
        return jnp.zeros_like(x[0]) if out is None else out

    result = []
    for a in range(COARSE):
        cos = lambda s: math.cos(2 * math.pi * s * a / 16)
        sin = lambda s: math.sin(2 * math.pi * s * a / 16)
        even, odd = (plus, minus) if a % 2 == 0 else (minus, plus)
        re = total([(1.0, x[0]), (cos(4), x[4])] + [(cos(s), even[s]) for s in (1, 2, 3)])
        im = total([(-sin(4), x[4])] + [(-sin(s), odd[s]) for s in (1, 2, 3)])
        result.append((re, im))
    return result


def kernel(
    sig_in, gat_in, fil_in, skip_in, w, test_in, turn_in, left_in, fwd_in, inv_in,
    mixed, out_y, out_z,
    sig, gat, fil, skip, turn, left, fwd, inv, sem_in,
    send_a, recv_a, send_b, recv_b, depth, w_group, part, recv_p, spec, back,
    test, w_rows, send_v, recv_v, v_own, v_near, send_y, recv_y, full_y, last_y,
    part_z, send_z, recv_z, recv_h, full_z,
    sem_a, sem_b, sem_g, sem_w, sem_r, sem_e, sem_v, sem_u, sem_p, sem_q, sem_y, sem_c, sem_h, sem_f, sem_k,
):
    me_s, me_c = lax.axis_index("seq"), lax.axis_index("chan")
    group, near, core = me_c // NEAR, me_c % NEAR, me_s % 2

    def on_seq(k):
        return {"seq": lax.rem(me_s + k, SEQ_DEV), "chan": me_c}

    def on_chan(k):
        return {"seq": me_s, "chan": lax.rem(me_c + k, CHAN_DEV)}

    def on_near(k):
        return {"seq": me_s, "chan": group * NEAR + lax.rem(near + k, NEAR)}

    def on_far(k):
        return {"seq": me_s, "chan": lax.rem(me_c + NEAR * k, CHAN_DEV)}

    other_core = {"seq": me_s + 1 - 2 * core, "chan": me_c}

    def remote(src, dst, sems, k, target):
        copy = pltpu.make_async_remote_copy(
            src_ref=src, dst_ref=dst, send_sem=sems.at[0, k], recv_sem=sems.at[1, k],
            device_id=target, device_id_type=MESH,
        )
        copy.start()
        return copy

    def local(k, src, dst):
        copy = pltpu.make_async_copy(src, dst, sem_in.at[k])
        copy.start()
        return copy

    def finish(*groups):
        for copies in groups:
            for copy in copies:
                copy.wait()

    in_sig = [local(0, sig_in, sig), local(1, fil_in, fil)]
    in_tables = [
        local(2, fwd_in, fwd), local(3, turn_in, turn), local(4, left_in, left), local(5, inv_in, inv)
    ]
    in_gate = [local(6, gat_in, gat), local(7, skip_in, skip)]

    barrier = pltpu.get_barrier_semaphore()
    for k in range(1, SEQ_DEV):
        pl.semaphore_signal(barrier, inc=1, device_id=on_seq(k), device_id_type=MESH)
    for k in range(1, CHAN_DEV):
        pl.semaphore_signal(barrier, inc=1, device_id=on_chan(k), device_id_type=MESH)

    finish(in_sig)
    for at, source in enumerate((sig, fil)):
        blocks = [source[q * SUB : (q + 1) * SUB, :].astype(F32) for q in range(8)]
        for d, block in enumerate(block_transpose(blocks)):
            send_a[d, at * SUB : (at + 1) * SUB, :] = block.astype(BF16)

    pl.semaphore_wait(barrier, SEQ_DEV - 1 + CHAN_DEV - 1)

    copies_a = [
        remote(send_a.at[lax.rem(me_s + k, SEQ_DEV)], recv_a.at[me_s], sem_a, k, on_seq(k))
        for k in SEQ_ORDER
    ]

    columns = pl.ds(pl.multiple_of(group * CHANS, CHANS), CHANS)
    copies_e, copies_r, copies_w = [], [], []

    def weight_rows(target, first, count):
        return pl.ds(pl.multiple_of(target * NEAR * CHANS + first, CHANS), count)

    for k in range(1, FAR):
        rows = weight_rows(lax.rem(group + k, FAR), me_s * CHANS, CHANS)
        copies_r.append(remote(w.at[rows, :], w_rows.at[:, columns], sem_r, k, on_far(k)))
        copies_e.append(remote(test_in, test.at[group], sem_e, k, on_far(k)))
    copies_r.append(local(8, w.at[weight_rows(group, me_s * CHANS, CHANS), :], w_rows.at[:, columns]))
    copies_e.append(local(9, test_in, test.at[group]))
    half_rows = pl.ds(pl.multiple_of(core * WEIGHT_HALF, WEIGHT_HALF), WEIGHT_HALF)
    w_half = w_group.at[half_rows, :]
    for k in range(1, FAR):
        rows = weight_rows(lax.rem(group + k, FAR), core * WEIGHT_HALF, WEIGHT_HALF)
        copies_w.append(remote(w.at[rows, :], w_group.at[half_rows, columns], sem_w, k, on_far(k)))
    rows = weight_rows(group, core * WEIGHT_HALF, WEIGHT_HALF)
    copies_w.append(local(10, w.at[rows, :], w_group.at[half_rows, columns]))
    recv_a[me_s] = send_a[me_s]

    finish(copies_r, copies_e)
    product = jnp.zeros((CHANS, RANK), F32)
    for f in range(FAR):
        product = product + dot(w_rows[:, f * CHANS : (f + 1) * CHANS], test[f])
    send_v[...] = product.T.reshape(NEAR, SLICE, CHANS).astype(BF16)

    finish(copies_a)
    copies_v = [
        remote(send_v.at[lax.rem(near + k, NEAR)], recv_v.at[near], sem_v, k, on_near(k))
        for k in range(1, NEAR)
    ]
    recv_v[near] = send_v[near]
    finish(in_tables)
    for at in range(2):
        blocks = [recv_a[s, at * SUB : (at + 1) * SUB, :].astype(F32) for s in range(SEQ_DEV)]
        for a, (re, im) in enumerate(coarse_forward(blocks)):
            spec[a, at * SUB : (at + 1) * SUB, :128] = re
            spec[a, at * SUB : (at + 1) * SUB, 128:] = im
    for a in range(COARSE):
        high, low = split(spec[a])
        z = dot(high, fwd[0, a]) + dot(low, fwd[0, a]) + dot(high, fwd[1, a])
        cos, sin = turn[a, 0], turn[a, 1]
        halves = []
        for at in range(2):
            re, im = z[at * SUB : (at + 1) * SUB, :128], z[at * SUB : (at + 1) * SUB, 128:]
            halves.append(jnp.concatenate([re * cos + im * sin, im * cos - re * sin], 0))
        high, low = split(jnp.concatenate(halves, 1))
        f = dot(left[0], jnp.concatenate([high, low, high], 0))
        sr, si, fr, fi = f[:SUB, :128], f[SUB:, :128], f[:SUB, 128:], f[SUB:, 128:]
        high, low = split(jnp.concatenate([sr * fr - si * fi, sr * fi + si * fr], 0))
        g = dot(left[1], jnp.concatenate([high, low, high], 0))
        re, im = g[:SUB], g[SUB:]
        high, low = split(jnp.concatenate([re * cos - im * sin, im * cos + re * sin], 1))
        back[a] = dot(high, inv[0, a]) + dot(low, inv[0, a]) + dot(high, inv[1, a])
    for s in range(5):
        sums = {}
        for a in range(COARSE):
            cos, sin = math.cos(2 * math.pi * s * a / 16), math.sin(2 * math.pi * s * a / 16)
            for name, factor, lanes in (("c", cos, 0), ("s", sin, 128)):
                if abs(factor) > 1e-9:
                    term = back[a, :, lanes : lanes + 128] * np.float32(factor)
                    key = name + "eo"[a % 2]
                    sums[key] = sums[key] + term if key in sums else term
        zero = jnp.zeros((SUB, 128), F32)
        ce, co, se, so = (sums.get(key, zero) for key in ("ce", "co", "se", "so"))
        send_b[s] = (ce + co - se - so).astype(BF16)
        if s in (1, 2, 3):
            send_b[8 - s] = (ce - co + se - so).astype(BF16)

    copies_b = [
        remote(send_b.at[lax.rem(me_s + k, SEQ_DEV)], recv_b.at[me_s], sem_b, k, on_seq(k))
        for k in SEQ_ORDER
    ]
    recv_b[me_s] = send_b[me_s]
    finish(copies_v)
    total = recv_v[0].astype(F32)
    for n in range(1, NEAR):
        total = total + recv_v[n].astype(F32)
    v_own[...] = total.astype(BF16)
    v_lanes = pl.ds(pl.multiple_of(me_s * CHANS, CHANS), CHANS)
    copies_u = [remote(v_own, v_near.at[:, v_lanes], sem_u, k, on_seq(k)) for k in SEQ_ORDER]
    v_near[:, v_lanes] = v_own[...]
    finish(copies_w)
    copies_k = [remote(w_half, w_half, sem_k, 0, other_core)]
    finish(in_gate, copies_b)
    near_columns = pl.ds(pl.multiple_of(near * CHANS, CHANS), CHANS)
    convolved = block_transpose([recv_b[d].astype(F32) for d in range(8)])
    copies_g = []
    for i in range(CHUNKS):
        for q in range(i * 8 // CHUNKS, (i + 1) * 8 // CHUNKS):
            rows = slice(q * SUB, (q + 1) * SUB)
            value = convolved[q] + skip[...] * sig[rows, :].astype(F32)
            depth[rows, near_columns] = (gat[rows, :].astype(F32) * value).astype(BF16)
        block = depth.at[i * STEP : (i + 1) * STEP, near_columns]
        copies_g.append([remote(block, block, sem_g, i * NEAR + k, on_near(k)) for k in range(1, NEAR)])

    copies_p, copies_q, copies_y = [], [], []
    y_rows = pl.ds(pl.multiple_of((near * FAR + group) * 8, 8), 8)

    def sum_y():
        finish(copies_q)
        total = recv_y[0]
        for f in range(1, FAR):
            total = total + recv_y[f]
        full_y[y_rows, :HALF] = total
        block = full_y.at[y_rows, :HALF]
        copies_y.append([remote(block, block, sem_y, k, on_chan(k)) for k in range(1, CHAN_DEV)])

    finish(copies_k, copies_u)
    for i in range(CHUNKS):
        rows = slice(i * STEP, (i + 1) * STEP)
        if i == CHUNKS - 1:
            sum_y()
        finish(copies_g[i])
        block = depth[rows, :]
        sketch = lax.dot_general(
            v_near[...], block, (((1,), (1,)), ((), ())), preferred_element_type=F32
        )
        if i < CHUNKS // 2:
            for f in range(FAR):
                send_y[f, :, rows] = sketch[f * 8 : (f + 1) * 8, :]
        else:
            last_y[i % 2, me_c] = sketch.astype(BF16)
            own = last_y.at[i % 2, me_c]
            first = (i - 1) * CHAN_DEV
            copies_y.append([remote(own, own, sem_y, first + k, on_chan(k)) for k in range(1, CHAN_DEV)])
        if i == CHUNKS // 2 - 1:
            copies_q = [
                remote(send_y.at[lax.rem(group + k, FAR)], recv_y.at[group], sem_q, k, on_far(k))
                for k in range(1, FAR)
            ]
            recv_y[group] = send_y[group]
        projected = dot(block, w_group[...])
        for f in range(FAR):
            part[f, rows, :] = projected[:, f * CHANS : (f + 1) * CHANS].astype(BF16)
        copies_p.append(
            [
                remote(
                    part.at[lax.rem(group + k, FAR), rows, :], recv_p.at[group, rows, :],
                    sem_p, i * FAR + k, on_far(k),
                )
                for k in range(1, FAR)
            ]
        )
        recv_p[group, rows, :] = part[group, rows, :]
    for i in range(CHUNKS):
        rows = slice(i * STEP, (i + 1) * STEP)
        finish(copies_p[i])
        total = recv_p[0, rows, :].astype(F32)
        for f in range(1, FAR):
            total = total + recv_p[f, rows, :].astype(F32)
        mixed[rows, :] = total.astype(BF16)

    finish(*copies_y)
    for i in range(CHUNKS // 2, CHUNKS):
        total = last_y[i % 2, :NEAR].astype(F32)
        for f in range(1, FAR):
            total = total + last_y[i % 2, f * NEAR : (f + 1) * NEAR].astype(F32)
        full_y[:, i * STEP : (i + 1) * STEP] = total.reshape(RANK, STEP)
    sum_z = dot(full_y[...].astype(BF16), mixed[...])
    part_z[...] = (sum_z * np.float32(1.0 / (SEQ_DEV * ROWS))).reshape(2, CHANS, CHANS)
    send_z[...] = part_z[1 - core].astype(BF16)
    copies_c = [remote(send_z, recv_z, sem_c, 0, other_core)]
    finish(copies_c)
    high = me_s // 2
    recv_h[high] = (part_z[core] + recv_z[...].astype(F32)).astype(BF16)
    copies_h = [remote(recv_h.at[high], recv_h.at[high], sem_h, k, on_seq(2 * k)) for k in (2, 1, 3)]
    out_y[...] = full_y[...].T
    finish(copies_h)
    total = recv_h[0].astype(F32)
    for h in range(1, 4):
        total = total + recv_h[h].astype(F32)
    full_z[core] = total.astype(BF16)
    copies_f = [remote(full_z.at[core], full_z.at[core], sem_f, 0, other_core)]
    finish(copies_f)
    out_z[...] = full_z[...].reshape(RANK, CHANS).astype(F32).T


def store(*refs):
    ins, outs, held, sems = refs[:3], refs[3:6], refs[6:9], refs[9]
    first = [pltpu.make_async_copy(a, b, sems.at[0, k]) for k, (a, b) in enumerate(zip(ins, held))]
    second = [pltpu.make_async_copy(a, b, sems.at[1, k]) for k, (a, b) in enumerate(zip(held, outs))]
    for copy in first:
        copy.start()
    for k in range(3):
        first[k].wait()
        second[k].start()
    for copy in second:
        copy.wait()


def per_device(signal, gating, filter_taps, skip_bias, out_weight, test_matrix):
    vmem = pl.BlockSpec(memory_space=pltpu.VMEM)
    constants = [jnp.asarray(t) for t in tables()]
    args = [signal, gating, filter_taps, skip_bias[None, :], out_weight, test_matrix] + constants
    outs = (
        jax.ShapeDtypeStruct((ROWS, CHANS), BF16),
        jax.ShapeDtypeStruct((ROWS, RANK), F32),
        jax.ShapeDtypeStruct((CHANS, RANK), F32),
    )

    def sems(n):
        return pltpu.SemaphoreType.DMA((2, n))

    results = pl.pallas_call(
        kernel,
        out_shape=outs,
        in_specs=[pl.BlockSpec(memory_space=pl.ANY)] * len(args),
        out_specs=(vmem, vmem, vmem),
        scratch_shapes=[
            pltpu.VMEM((ROWS, CHANS), BF16),
            pltpu.VMEM((ROWS, CHANS), BF16),
            pltpu.VMEM((ROWS, CHANS), BF16),
            pltpu.VMEM((1, CHANS), F32),
        ]
        + [pltpu.VMEM(c.shape, c.dtype) for c in constants]
        + [
            pltpu.SemaphoreType.DMA((11,)),
            pltpu.VMEM((SEQ_DEV, 2 * SUB, 128), BF16),
            pltpu.VMEM((SEQ_DEV, 2 * SUB, 128), BF16),
            pltpu.VMEM((SEQ_DEV, SUB, 128), BF16),
            pltpu.VMEM((SEQ_DEV, SUB, 128), BF16),
            pltpu.VMEM((ROWS, NEAR * CHANS), BF16),
            pltpu.VMEM((NEAR * CHANS, FAR * CHANS), BF16),
            pltpu.VMEM((FAR, ROWS, CHANS), BF16),
            pltpu.VMEM((FAR, ROWS, CHANS), BF16),
            pltpu.VMEM((COARSE, 2 * SUB, 256), F32),
            pltpu.VMEM((COARSE, SUB, 256), F32),
            pltpu.VMEM((FAR, CHANS, RANK), BF16),
            pltpu.VMEM((CHANS, FAR * CHANS), BF16),
            pltpu.VMEM((NEAR, SLICE, CHANS), BF16),
            pltpu.VMEM((NEAR, SLICE, CHANS), BF16),
            pltpu.VMEM((SLICE, CHANS), BF16),
            pltpu.VMEM((SLICE, NEAR * CHANS), BF16),
            pltpu.VMEM((FAR, 8, HALF), F32),
            pltpu.VMEM((FAR, 8, HALF), F32),
            pltpu.VMEM((RANK, ROWS), F32),
            pltpu.VMEM((2, CHAN_DEV, SLICE, STEP), BF16),
            pltpu.VMEM((2, CHANS, CHANS), F32),
            pltpu.VMEM((CHANS, CHANS), BF16),
            pltpu.VMEM((CHANS, CHANS), BF16),
            pltpu.VMEM((4, CHANS, CHANS), BF16),
            pltpu.VMEM((2, CHANS, CHANS), BF16),
            sems(SEQ_DEV), sems(SEQ_DEV), sems(CHUNKS * NEAR), sems(FAR), sems(FAR), sems(FAR),
            sems(NEAR), sems(SEQ_DEV), sems(CHUNKS * FAR), sems(FAR), sems(3 * CHAN_DEV),
            sems(1), sems(4), sems(1), sems(1),
        ],
        compiler_params=pltpu.CompilerParams(
            collective_id=0, has_side_effects=True, vmem_limit_bytes=60 * 2**20
        ),
    )(*args)
    return pl.pallas_call(
        store,
        out_shape=outs,
        in_specs=[pl.BlockSpec(memory_space=pl.ANY)] * 3,
        out_specs=(pl.BlockSpec(memory_space=pl.ANY),) * 3,
        scratch_shapes=[pltpu.VMEM(o.shape, o.dtype) for o in outs]
        + [pltpu.SemaphoreType.DMA((2, 3))],
        compiler_params=pltpu.CompilerParams(vmem_limit_bytes=60 * 2**20),
    )(*results)


def solution(mesh):
    return jax.shard_map(
        per_device,
        mesh=mesh,
        in_specs=(
            P("seq", "chan"), P("seq", "chan"), P("seq", "chan"),
            P("chan"), P(None, "chan"), P("chan", None),
        ),
        out_specs=(P("seq", "chan"), P("seq", None), P("chan", None)),
        check_vma=False,
    )
```

```python
import functools
import math

import jax
import jax.numpy as jnp
import numpy as np
from jax import lax
from jax.experimental import pallas as pl
from jax.experimental.pallas import tpu as pltpu
from jax.sharding import PartitionSpec as P

MESH = pl.DeviceIdType.MESH
F32, BF16 = jnp.float32, jnp.bfloat16

SEQ_DEV = 8
CHAN_DEV = 32
NEAR = 8
FAR = 4
ROWS = 512
CHANS = 128
SUB = 64
LANES = 16
COARSE = 9
RANK = 256
SLICE = RANK // NEAR
CHUNKS = 4
STEP = ROWS // CHUNKS
WEIGHT_HALF = NEAR * CHANS // 2
SEQ_ORDER = (4, 3, 5, 2, 6, 1, 7)


def split_np(x):
    high = x.astype(jnp.bfloat16)
    low = (x - high.astype(np.float64)).astype(jnp.bfloat16)
    return high, low


@functools.lru_cache(None)
def tables():
    n = 2 * SEQ_DEV * ROWS
    j = np.arange(SUB)
    q = np.arange(8)
    b = np.arange(8)
    turn = []
    fwd, inv = [], []
    eye = np.eye(LANES)
    for a in range(COARSE):
        k1 = a + 16 * b
        angle = 2 * np.pi * np.outer(j, k1) / n
        turn.append((np.repeat(np.cos(angle), LANES, 1), np.repeat(np.sin(angle), LANES, 1)))
        ang = 2 * np.pi * np.outer(q, k1) / 128
        c, s = np.kron(np.cos(ang), eye), np.kron(np.sin(ang), eye)
        fwd.append(np.block([[c, -s], [s, c]]))
        weight = (1.0 if a in (0, 8) else 2.0) / n
        inv.append(np.block([[c.T, s.T], [-s.T, c.T]]) * weight)
    fine = 2 * np.pi * np.outer(j, j) / SUB
    c, s = np.cos(fine), np.sin(fine)
    left = np.block([[c, s], [-s, c]])
    left_inv = np.block([[c, -s], [s, c]])

    def triple(m):
        high, low = split_np(m)
        return np.concatenate([high, high, low], 1)

    fwd = np.stack(split_np(np.stack(fwd)))
    inv = np.stack(split_np(np.stack(inv)))
    turn = np.stack([np.stack(t) for t in turn]).astype(np.float32)
    return turn, np.stack([triple(left), triple(left_inv)]), fwd, inv


def dot(a, b):
    return lax.dot_general(a, b, (((1,), (0,)), ((), ())), preferred_element_type=F32)


def split(x):
    high = x.astype(BF16)
    return high, (x - high.astype(F32)).astype(BF16)


def block_transpose(blocks):
    lane = lax.broadcasted_iota(jnp.int32, (SUB, 128), 1)
    for bit in range(3):
        step = LANES << bit
        low = (lane & step) == 0
        new = list(blocks)
        for q in range(8):
            if q >> bit & 1:
                continue
            p = q | 1 << bit
            new[q] = jnp.where(low, blocks[q], pltpu.roll(blocks[p], step, 1))
            new[p] = jnp.where(low, pltpu.roll(blocks[q], 128 - step, 1), blocks[p])
        blocks = new
    return blocks


def coarse_forward(x):
    plus = {s: x[s] + x[8 - s] for s in (1, 2, 3)}
    minus = {s: x[s] - x[8 - s] for s in (1, 2, 3)}

    def total(terms):
        out = None
        for factor, value in terms:
            if abs(factor) < 1e-9:
                continue
            if abs(factor - 1) < 1e-9:
                term = value
            elif abs(factor + 1) < 1e-9:
                term = -value
            else:
                term = value * np.float32(factor)
            out = term if out is None else out + term
        return jnp.zeros_like(x[0]) if out is None else out

    result = []
    for a in range(COARSE):
        cos = lambda s: math.cos(2 * math.pi * s * a / 16)
        sin = lambda s: math.sin(2 * math.pi * s * a / 16)
        even, odd = (plus, minus) if a % 2 == 0 else (minus, plus)
        re = total([(1.0, x[0]), (cos(4), x[4])] + [(cos(s), even[s]) for s in (1, 2, 3)])
        im = total([(-sin(4), x[4])] + [(-sin(s), odd[s]) for s in (1, 2, 3)])
        result.append((re, im))
    return result


def kernel(
    sig_in, gat_in, fil_in, skip_in, w, test_in, turn_in, left_in, fwd_in, inv_in,
    mixed, out_y, out_z,
    sig, gat, fil, skip, turn, left, fwd, inv, sem_in,
    send_a, recv_a, send_b, recv_b, depth, w_group, part, recv_p, spec, back,
    test, w_rows, send_v, recv_v, v_own, v_near, part_y, near_y,
    part_z, send_z, recv_z, recv_h, full_z,
    sem_a, sem_b, sem_g, sem_w, sem_r, sem_e, sem_v, sem_u, sem_p, sem_q, sem_y, sem_c, sem_h, sem_f, sem_k,
):
    me_s, me_c = lax.axis_index("seq"), lax.axis_index("chan")
    group, near, core = me_c // NEAR, me_c % NEAR, me_s % 2

    def on_seq(k):
        return {"seq": lax.rem(me_s + k, SEQ_DEV), "chan": me_c}

    def on_near(k):
        return {"seq": me_s, "chan": group * NEAR + lax.rem(near + k, NEAR)}

    def on_far(k):
        return {"seq": me_s, "chan": lax.rem(me_c + NEAR * k, CHAN_DEV)}

    other_core = {"seq": me_s + 1 - 2 * core, "chan": me_c}

    def remote(src, dst, sems, k, target):
        copy = pltpu.make_async_remote_copy(
            src_ref=src, dst_ref=dst, send_sem=sems.at[0, k], recv_sem=sems.at[1, k],
            device_id=target, device_id_type=MESH,
        )
        copy.start()
        return copy

    def local(k, src, dst):
        copy = pltpu.make_async_copy(src, dst, sem_in.at[k])
        copy.start()
        return copy

    def finish(*groups):
        for copies in groups:
            for copy in copies:
                copy.wait()

    in_sig = [local(0, sig_in, sig), local(1, fil_in, fil)]
    in_tables = [
        local(2, fwd_in, fwd), local(3, turn_in, turn), local(4, left_in, left), local(5, inv_in, inv)
    ]
    in_gate = [local(6, gat_in, gat), local(7, skip_in, skip)]

    barrier = pltpu.get_barrier_semaphore()
    for k in range(1, SEQ_DEV):
        pl.semaphore_signal(barrier, inc=1, device_id=on_seq(k), device_id_type=MESH)
    for k in range(1, NEAR):
        pl.semaphore_signal(barrier, inc=1, device_id=on_near(k), device_id_type=MESH)
    for k in range(1, FAR):
        pl.semaphore_signal(barrier, inc=1, device_id=on_far(k), device_id_type=MESH)

    finish(in_sig)
    for at, source in enumerate((sig, fil)):
        blocks = [source[q * SUB : (q + 1) * SUB, :].astype(F32) for q in range(8)]
        for d, block in enumerate(block_transpose(blocks)):
            send_a[d, at * SUB : (at + 1) * SUB, :] = block.astype(BF16)

    pl.semaphore_wait(barrier, SEQ_DEV - 1 + NEAR - 1 + FAR - 1)

    copies_a = [
        remote(send_a.at[lax.rem(me_s + k, SEQ_DEV)], recv_a.at[me_s], sem_a, k, on_seq(k))
        for k in SEQ_ORDER
    ]

    columns = pl.ds(pl.multiple_of(group * CHANS, CHANS), CHANS)
    copies_e, copies_r, copies_w = [], [], []

    def weight_rows(target, first, count):
        return pl.ds(pl.multiple_of(target * NEAR * CHANS + first, CHANS), count)

    for k in range(1, FAR):
        rows = weight_rows(lax.rem(group + k, FAR), me_s * CHANS, CHANS)
        copies_r.append(remote(w.at[rows, :], w_rows.at[:, columns], sem_r, k, on_far(k)))
        copies_e.append(remote(test_in, test.at[group], sem_e, k, on_far(k)))
    copies_r.append(local(8, w.at[weight_rows(group, me_s * CHANS, CHANS), :], w_rows.at[:, columns]))
    copies_e.append(local(9, test_in, test.at[group]))
    half_rows = pl.ds(pl.multiple_of(core * WEIGHT_HALF, WEIGHT_HALF), WEIGHT_HALF)
    w_half = w_group.at[half_rows, :]
    for k in range(1, FAR):
        rows = weight_rows(lax.rem(group + k, FAR), core * WEIGHT_HALF, WEIGHT_HALF)
        copies_w.append(remote(w.at[rows, :], w_group.at[half_rows, columns], sem_w, k, on_far(k)))
    rows = weight_rows(group, core * WEIGHT_HALF, WEIGHT_HALF)
    copies_w.append(local(10, w.at[rows, :], w_group.at[half_rows, columns]))
    recv_a[me_s] = send_a[me_s]

    finish(copies_r, copies_e)
    product = jnp.zeros((CHANS, RANK), F32)
    for f in range(FAR):
        product = product + dot(w_rows[:, f * CHANS : (f + 1) * CHANS], test[f])
    send_v[...] = product.T.reshape(NEAR, SLICE, CHANS).astype(BF16)

    finish(copies_a)
    copies_v = [
        remote(send_v.at[lax.rem(near + k, NEAR)], recv_v.at[near], sem_v, k, on_near(k))
        for k in range(1, NEAR)
    ]
    recv_v[near] = send_v[near]
    finish(in_tables)
    for at in range(2):
        blocks = [recv_a[s, at * SUB : (at + 1) * SUB, :].astype(F32) for s in range(SEQ_DEV)]
        for a, (re, im) in enumerate(coarse_forward(blocks)):
            spec[a, at * SUB : (at + 1) * SUB, :128] = re
            spec[a, at * SUB : (at + 1) * SUB, 128:] = im
    for a in range(COARSE):
        high, low = split(spec[a])
        z = dot(high, fwd[0, a]) + dot(low, fwd[0, a]) + dot(high, fwd[1, a])
        cos, sin = turn[a, 0], turn[a, 1]
        halves = []
        for at in range(2):
            re, im = z[at * SUB : (at + 1) * SUB, :128], z[at * SUB : (at + 1) * SUB, 128:]
            halves.append(jnp.concatenate([re * cos + im * sin, im * cos - re * sin], 0))
        high, low = split(jnp.concatenate(halves, 1))
        f = dot(left[0], jnp.concatenate([high, low, high], 0))
        sr, si, fr, fi = f[:SUB, :128], f[SUB:, :128], f[:SUB, 128:], f[SUB:, 128:]
        high, low = split(jnp.concatenate([sr * fr - si * fi, sr * fi + si * fr], 0))
        g = dot(left[1], jnp.concatenate([high, low, high], 0))
        re, im = g[:SUB], g[SUB:]
        high, low = split(jnp.concatenate([re * cos - im * sin, im * cos + re * sin], 1))
        back[a] = dot(high, inv[0, a]) + dot(low, inv[0, a]) + dot(high, inv[1, a])
    for s in range(5):
        sums = {}
        for a in range(COARSE):
            cos, sin = math.cos(2 * math.pi * s * a / 16), math.sin(2 * math.pi * s * a / 16)
            for name, factor, lanes in (("c", cos, 0), ("s", sin, 128)):
                if abs(factor) > 1e-9:
                    term = back[a, :, lanes : lanes + 128] * np.float32(factor)
                    key = name + "eo"[a % 2]
                    sums[key] = sums[key] + term if key in sums else term
        zero = jnp.zeros((SUB, 128), F32)
        ce, co, se, so = (sums.get(key, zero) for key in ("ce", "co", "se", "so"))
        send_b[s] = (ce + co - se - so).astype(BF16)
        if s in (1, 2, 3):
            send_b[8 - s] = (ce - co + se - so).astype(BF16)

    copies_b = [
        remote(send_b.at[lax.rem(me_s + k, SEQ_DEV)], recv_b.at[me_s], sem_b, k, on_seq(k))
        for k in SEQ_ORDER
    ]
    recv_b[me_s] = send_b[me_s]
    finish(copies_v)
    total = recv_v[0].astype(F32)
    for n in range(1, NEAR):
        total = total + recv_v[n].astype(F32)
    v_own[...] = total.astype(BF16)
    v_lanes = pl.ds(pl.multiple_of(me_s * CHANS, CHANS), CHANS)
    copies_u = [remote(v_own, v_near.at[:, v_lanes], sem_u, k, on_seq(k)) for k in SEQ_ORDER]
    v_near[:, v_lanes] = v_own[...]
    finish(copies_w)
    copies_k = [remote(w_half, w_half, sem_k, 0, other_core)]
    finish(in_gate, copies_b)
    near_columns = pl.ds(pl.multiple_of(near * CHANS, CHANS), CHANS)
    convolved = block_transpose([recv_b[d].astype(F32) for d in range(8)])
    copies_g = []
    for i in range(CHUNKS):
        for q in range(i * 8 // CHUNKS, (i + 1) * 8 // CHUNKS):
            rows = slice(q * SUB, (q + 1) * SUB)
            value = convolved[q] + skip[...] * sig[rows, :].astype(F32)
            depth[rows, near_columns] = (gat[rows, :].astype(F32) * value).astype(BF16)
        block = depth.at[i * STEP : (i + 1) * STEP, near_columns]
        copies_g.append([remote(block, block, sem_g, i * NEAR + k, on_near(k)) for k in range(1, NEAR)])

    copies_p, copies_q, copies_y = [], [], []

    def sum_y(i):
        finish(copies_q[i])
        total = part_y[i, 0]
        for f in range(1, FAR):
            total = total + part_y[i, f]
        near_y[i, near] = total.astype(BF16)
        own = near_y.at[i, near]
        copies_y.append([remote(own, own, sem_y, i * NEAR + k, on_near(k)) for k in range(1, NEAR)])

    finish(copies_k, copies_u)
    for i in range(CHUNKS):
        rows = slice(i * STEP, (i + 1) * STEP)
        finish(copies_g[i])
        block = depth[rows, :]
        part_y[i, group] = lax.dot_general(
            v_near[...], block, (((1,), (1,)), ((), ())), preferred_element_type=F32
        )
        own = part_y.at[i, group]
        copies_q.append([remote(own, own, sem_q, i * FAR + k, on_far(k)) for k in range(1, FAR)])
        projected = dot(block, w_group[...])
        for f in range(FAR):
            part[f, rows, :] = projected[:, f * CHANS : (f + 1) * CHANS].astype(BF16)
        copies_p.append(
            [
                remote(
                    part.at[lax.rem(group + k, FAR), rows, :], recv_p.at[group, rows, :],
                    sem_p, i * FAR + k, on_far(k),
                )
                for k in range(1, FAR)
            ]
        )
        recv_p[group, rows, :] = part[group, rows, :]
        if i:
            sum_y(i - 1)
    sum_y(CHUNKS - 1)
    for i in range(CHUNKS):
        rows = slice(i * STEP, (i + 1) * STEP)
        finish(copies_p[i])
        total = recv_p[0, rows, :].astype(F32)
        for f in range(1, FAR):
            total = total + recv_p[f, rows, :].astype(F32)
        mixed[rows, :] = total.astype(BF16)

    sum_z = jnp.zeros((RANK, CHANS), F32)
    for i in range(CHUNKS):
        finish(copies_y[i])
        sum_z = sum_z + dot(near_y[i].reshape(RANK, STEP), mixed[i * STEP : (i + 1) * STEP, :])
    part_z[...] = (sum_z * np.float32(1.0 / (SEQ_DEV * ROWS))).reshape(2, CHANS, CHANS)
    send_z[...] = part_z[1 - core].astype(BF16)
    copies_c = [remote(send_z, recv_z, sem_c, 0, other_core)]
    finish(copies_c)
    high = me_s // 2
    recv_h[high] = (part_z[core] + recv_z[...].astype(F32)).astype(BF16)
    copies_h = [remote(recv_h.at[high], recv_h.at[high], sem_h, k, on_seq(2 * k)) for k in (2, 1, 3)]
    for i in range(CHUNKS):
        out_y[i * STEP : (i + 1) * STEP, :] = near_y[i].reshape(RANK, STEP).astype(F32).T
    finish(copies_h)
    total = recv_h[0].astype(F32)
    for h in range(1, 4):
        total = total + recv_h[h].astype(F32)
    full_z[core] = total.astype(BF16)
    copies_f = [remote(full_z.at[core], full_z.at[core], sem_f, 0, other_core)]
    finish(copies_f)
    out_z[...] = full_z[...].reshape(RANK, CHANS).astype(F32).T


def store(*refs):
    ins, outs, held, sems = refs[:3], refs[3:6], refs[6:9], refs[9]
    first = [pltpu.make_async_copy(a, b, sems.at[0, k]) for k, (a, b) in enumerate(zip(ins, held))]
    second = [pltpu.make_async_copy(a, b, sems.at[1, k]) for k, (a, b) in enumerate(zip(held, outs))]
    for copy in first:
        copy.start()
    for k in range(3):
        first[k].wait()
        second[k].start()
    for copy in second:
        copy.wait()


def per_device(signal, gating, filter_taps, skip_bias, out_weight, test_matrix):
    vmem = pl.BlockSpec(memory_space=pltpu.VMEM)
    constants = [jnp.asarray(t) for t in tables()]
    args = [signal, gating, filter_taps, skip_bias[None, :], out_weight, test_matrix] + constants
    outs = (
        jax.ShapeDtypeStruct((ROWS, CHANS), BF16),
        jax.ShapeDtypeStruct((ROWS, RANK), F32),
        jax.ShapeDtypeStruct((CHANS, RANK), F32),
    )

    def sems(n):
        return pltpu.SemaphoreType.DMA((2, n))

    results = pl.pallas_call(
        kernel,
        out_shape=outs,
        in_specs=[pl.BlockSpec(memory_space=pl.ANY)] * len(args),
        out_specs=(vmem, vmem, vmem),
        scratch_shapes=[
            pltpu.VMEM((ROWS, CHANS), BF16),
            pltpu.VMEM((ROWS, CHANS), BF16),
            pltpu.VMEM((ROWS, CHANS), BF16),
            pltpu.VMEM((1, CHANS), F32),
        ]
        + [pltpu.VMEM(c.shape, c.dtype) for c in constants]
        + [
            pltpu.SemaphoreType.DMA((11,)),
            pltpu.VMEM((SEQ_DEV, 2 * SUB, 128), BF16),
            pltpu.VMEM((SEQ_DEV, 2 * SUB, 128), BF16),
            pltpu.VMEM((SEQ_DEV, SUB, 128), BF16),
            pltpu.VMEM((SEQ_DEV, SUB, 128), BF16),
            pltpu.VMEM((ROWS, NEAR * CHANS), BF16),
            pltpu.VMEM((NEAR * CHANS, FAR * CHANS), BF16),
            pltpu.VMEM((FAR, ROWS, CHANS), BF16),
            pltpu.VMEM((FAR, ROWS, CHANS), BF16),
            pltpu.VMEM((COARSE, 2 * SUB, 256), F32),
            pltpu.VMEM((COARSE, SUB, 256), F32),
            pltpu.VMEM((FAR, CHANS, RANK), BF16),
            pltpu.VMEM((CHANS, FAR * CHANS), BF16),
            pltpu.VMEM((NEAR, SLICE, CHANS), BF16),
            pltpu.VMEM((NEAR, SLICE, CHANS), BF16),
            pltpu.VMEM((SLICE, CHANS), BF16),
            pltpu.VMEM((SLICE, NEAR * CHANS), BF16),
            pltpu.VMEM((CHUNKS, FAR, SLICE, STEP), F32),
            pltpu.VMEM((CHUNKS, NEAR, SLICE, STEP), BF16),
            pltpu.VMEM((2, CHANS, CHANS), F32),
            pltpu.VMEM((CHANS, CHANS), BF16),
            pltpu.VMEM((CHANS, CHANS), BF16),
            pltpu.VMEM((4, CHANS, CHANS), BF16),
            pltpu.VMEM((2, CHANS, CHANS), BF16),
            sems(SEQ_DEV), sems(SEQ_DEV), sems(CHUNKS * NEAR), sems(FAR), sems(FAR), sems(FAR),
            sems(NEAR), sems(SEQ_DEV), sems(CHUNKS * FAR), sems(CHUNKS * FAR), sems(CHUNKS * NEAR),
            sems(1), sems(4), sems(1), sems(1),
        ],
        compiler_params=pltpu.CompilerParams(
            collective_id=0, has_side_effects=True, vmem_limit_bytes=60 * 2**20
        ),
    )(*args)
    return pl.pallas_call(
        store,
        out_shape=outs,
        in_specs=[pl.BlockSpec(memory_space=pl.ANY)] * 3,
        out_specs=(pl.BlockSpec(memory_space=pl.ANY),) * 3,
        scratch_shapes=[pltpu.VMEM(o.shape, o.dtype) for o in outs]
        + [pltpu.SemaphoreType.DMA((2, 3))],
        compiler_params=pltpu.CompilerParams(vmem_limit_bytes=60 * 2**20),
    )(*results)


def solution(mesh):
    return jax.shard_map(
        per_device,
        mesh=mesh,
        in_specs=(
            P("seq", "chan"), P("seq", "chan"), P("seq", "chan"),
            P("chan"), P(None, "chan"), P("chan", None),
        ),
        out_specs=(P("seq", "chan"), P("seq", None), P("chan", None)),
        check_vma=False,
    )
```

```python
import functools
import math

import jax
import jax.numpy as jnp
import numpy as np
from jax import lax
from jax.experimental import pallas as pl
from jax.experimental.pallas import tpu as pltpu
from jax.sharding import PartitionSpec as P

MESH = pl.DeviceIdType.MESH
F32, BF16 = jnp.float32, jnp.bfloat16

SEQ_DEV = 8
CHAN_DEV = 32
NEAR = 8
FAR = 4
ROWS = 512
CHANS = 128
SUB = 64
LANES = 16
COARSE = 9
RANK = 256
SLICE = RANK // NEAR
TOGETHER = 3
CHUNKS = 2
STEP = ROWS // CHUNKS
SEQ_ORDER = (4, 3, 5, 2, 6, 1, 7)


def split_np(x):
    high = x.astype(jnp.bfloat16)
    low = (x - high.astype(np.float64)).astype(jnp.bfloat16)
    return high, low


@functools.lru_cache(None)
def tables():
    n = 2 * SEQ_DEV * ROWS
    j = np.arange(SUB)
    q = np.arange(8)
    b = np.arange(8)
    turn = []
    fwd, inv = [], []
    eye = np.eye(LANES)
    for a in range(COARSE):
        k1 = a + 16 * b
        angle = 2 * np.pi * np.outer(j, k1) / n
        turn.append((np.repeat(np.cos(angle), LANES, 1), np.repeat(np.sin(angle), LANES, 1)))
        ang = 2 * np.pi * np.outer(q, k1) / 128
        c, s = np.kron(np.cos(ang), eye), np.kron(np.sin(ang), eye)
        fwd.append(np.block([[c, -s], [s, c]]))
        weight = (1.0 if a in (0, 8) else 2.0) / n
        inv.append(np.block([[c.T, s.T], [-s.T, c.T]]) * weight)
    fine = 2 * np.pi * np.outer(j, j) / SUB
    c, s = np.cos(fine), np.sin(fine)
    left = np.block([[c, s], [-s, c]])
    left_inv = np.block([[c, -s], [s, c]])

    def triple(m):
        high, low = split_np(m)
        return np.concatenate([high, high, low], 1)

    fwd = np.stack(split_np(np.stack(fwd)))
    inv = np.stack(split_np(np.stack(inv)))
    turn = np.stack([np.stack(t) for t in turn]).astype(np.float32)
    return turn, np.stack([triple(left), triple(left_inv)]), fwd, inv


def dot(a, b):
    return lax.dot_general(a, b, (((1,), (0,)), ((), ())), preferred_element_type=F32)


def split(x):
    high = x.astype(BF16)
    return high, (x - high.astype(F32)).astype(BF16)


def block_transpose(blocks):
    lane = lax.broadcasted_iota(jnp.int32, (SUB, 128), 1)
    for bit in range(3):
        step = LANES << bit
        low = (lane & step) == 0
        new = list(blocks)
        for q in range(8):
            if q >> bit & 1:
                continue
            p = q | 1 << bit
            new[q] = jnp.where(low, blocks[q], pltpu.roll(blocks[p], step, 1))
            new[p] = jnp.where(low, pltpu.roll(blocks[q], 128 - step, 1), blocks[p])
        blocks = new
    return blocks


def coarse_forward(x):
    plus = {s: x[s] + x[8 - s] for s in (1, 2, 3)}
    minus = {s: x[s] - x[8 - s] for s in (1, 2, 3)}

    def total(terms):
        out = None
        for factor, value in terms:
            if abs(factor) < 1e-9:
                continue
            if abs(factor - 1) < 1e-9:
                term = value
            elif abs(factor + 1) < 1e-9:
                term = -value
            else:
                term = value * np.float32(factor)
            out = term if out is None else out + term
        return jnp.zeros_like(x[0]) if out is None else out

    result = []
    for a in range(COARSE):
        cos = lambda s: math.cos(2 * math.pi * s * a / 16)
        sin = lambda s: math.sin(2 * math.pi * s * a / 16)
        even, odd = (plus, minus) if a % 2 == 0 else (minus, plus)
        re = total([(1.0, x[0]), (cos(4), x[4])] + [(cos(s), even[s]) for s in (1, 2, 3)])
        im = total([(-sin(4), x[4])] + [(-sin(s), odd[s]) for s in (1, 2, 3)])
        result.append((re, im))
    return result


def kernel(
    sig_in, gat_in, fil_in, skip_in, w, test_in, turn_in, left_in, fwd_in, inv_in,
    mixed, out_y, out_z,
    sig, gat, fil, skip, turn, left, fwd, inv, sem_in,
    send_a, recv_a, send_b, recv_b, depth, w_group, part, recv_p, spec, back,
    test, w_rows, send_v, recv_v, v_near, part_y, near_y,
    part_z, send_z, recv_z, recv_h, full_z,
    sem_a, sem_b, sem_g, sem_w, sem_r, sem_e, sem_v, sem_u, sem_p, sem_q, sem_y, sem_c, sem_h, sem_f, sem_k,
):
    me_s, me_c = lax.axis_index("seq"), lax.axis_index("chan")
    core = me_s % 2
    place = ((me_c // 2) % FAR, me_c // NEAR)
    beside = me_c % 2
    group = (place[1], place[0])
    member = (2 * place[0] + beside, 2 * place[1] + beside)

    def on_seq(k):
        return {"seq": lax.rem(me_s + k, SEQ_DEV), "chan": me_c}

    def on_line(o, k):
        at = lax.rem(place[o] + k, FAR)
        chan = NEAR * place[1] + 2 * at + beside if o == 0 else NEAR * at + 2 * place[0] + beside
        return {"seq": me_s, "chan": chan}

    def on_far(o, k):
        return on_line(1 - o, k)

    def on_member(o, k):
        at = lax.rem(member[o] + k, NEAR)
        chan = NEAR * place[1] + at if o == 0 else NEAR * (at // 2) + 2 * place[0] + at % 2
        return {"seq": me_s, "chan": chan}

    other_line = {"seq": me_s, "chan": me_c + 1 - 2 * beside}
    other_core = {"seq": me_s + 1 - 2 * core, "chan": me_c}

    def remote(src, dst, sems, k, target):
        copy = pltpu.make_async_remote_copy(
            src_ref=src, dst_ref=dst, send_sem=sems.at[0, k], recv_sem=sems.at[1, k],
            device_id=target, device_id_type=MESH,
        )
        copy.start()
        return copy

    def local(k, src, dst):
        copy = pltpu.make_async_copy(src, dst, sem_in.at[k])
        copy.start()
        return copy

    def finish(*groups):
        for copies in groups:
            for copy in copies:
                copy.wait()

    in_sig = [local(0, sig_in, sig), local(1, fil_in, fil)]
    in_tables = [
        local(2, fwd_in, fwd), local(3, turn_in, turn), local(4, left_in, left), local(5, inv_in, inv)
    ]
    in_gate = [local(6, gat_in, gat), local(7, skip_in, skip)]

    barrier = pltpu.get_barrier_semaphore()
    for k in range(1, SEQ_DEV):
        pl.semaphore_signal(barrier, inc=1, device_id=on_seq(k), device_id_type=MESH)
    for o in range(2):
        for k in range(1, NEAR):
            pl.semaphore_signal(barrier, inc=1, device_id=on_member(o, k), device_id_type=MESH)

    finish(in_sig)
    for at, source in enumerate((sig, fil)):
        blocks = [source[q * SUB : (q + 1) * SUB, :].astype(F32) for q in range(8)]
        for d, block in enumerate(block_transpose(blocks)):
            send_a[d, at * SUB : (at + 1) * SUB, :] = block.astype(BF16)

    pl.semaphore_wait(barrier, SEQ_DEV - 1 + 2 * (NEAR - 1))

    copies_a = [
        remote(send_a.at[lax.rem(me_s + k, SEQ_DEV)], recv_a.at[me_s], sem_a, k, on_seq(k))
        for k in SEQ_ORDER
    ]

    copies_e, copies_r, copies_w = [], [], []

    def weight(o, target, part, count):
        return w.at[target, pl.ds(part, count)] if o == 0 else w.at[pl.ds(part, count), target]

    def weight_rows(o, target):
        rows = pl.ds(pl.multiple_of(core * CHANS, CHANS), CHANS)
        return w.at[target, me_s // 2, rows] if o == 0 else w.at[me_s // 2, target, rows]

    columns = [pl.ds(pl.multiple_of(group[o] * CHANS, CHANS), CHANS) for o in range(2)]
    for o in range(2):
        for k in range(1, FAR):
            rows = weight_rows(o, lax.rem(group[o] + k, FAR))
            copies_r.append(
                remote(rows, w_rows.at[o, :, columns[o]], sem_r, o * FAR + k, on_far(o, k))
            )
            copies_e.append(remote(test_in, test.at[o, group[o]], sem_e, o * FAR + k, on_far(o, k)))
        copies_r.append(local(8 + o, weight_rows(o, group[o]), w_rows.at[o, :, columns[o]]))
        copies_e.append(local(10 + o, test_in, test.at[o, group[o]]))
    half = pl.ds(2 * core, 2)
    for o in range(2):
        target = w_group.at[o, half, :, columns[o]]
        for k in range(1, FAR):
            rows = weight(o, lax.rem(group[o] + k, FAR), 2 * core, 2)
            copies_w.append(remote(rows, target, sem_w, o * FAR + k, on_far(o, k)))
        copies_w.append(local(12 + o, weight(o, group[o], 2 * core, 2), target))
    recv_a[me_s] = send_a[me_s]

    finish(copies_r, copies_e)
    for o in range(2):
        product = jnp.zeros((CHANS, RANK), F32)
        for f in range(FAR):
            product = product + dot(w_rows[o, :, f * CHANS : (f + 1) * CHANS], test[o, f])
        send_v[o] = product.T.reshape(NEAR, SLICE, CHANS).astype(BF16)

    finish(copies_a)
    copies_v = []
    for o in range(2):
        for k in range(1, NEAR):
            block = send_v.at[o, lax.rem(member[o] + k, NEAR)]
            copies_v.append(
                remote(block, recv_v.at[o, member[o]], sem_v, o * NEAR + k, on_member(o, k))
            )
        recv_v[o, member[o]] = send_v[o, member[o]]
    finish(in_tables)
    for at in range(2):
        blocks = [recv_a[s, at * SUB : (at + 1) * SUB, :].astype(F32) for s in range(SEQ_DEV)]
        for a, (re, im) in enumerate(coarse_forward(blocks)):
            spec[a, at * SUB : (at + 1) * SUB, :128] = re
            spec[a, at * SUB : (at + 1) * SUB, 128:] = im
    for first in range(0, COARSE, TOGETHER):
        several = range(first, min(first + TOGETHER, COARSE))
        pairs = [split(spec[a]) for a in several]
        values = [
            dot(high, fwd[0, a]) + dot(low, fwd[0, a]) + dot(high, fwd[1, a])
            for a, (high, low) in zip(several, pairs)
        ]
        pairs = []
        for a, z in zip(several, values):
            cos, sin = turn[a, 0], turn[a, 1]
            halves = []
            for at in range(2):
                re, im = z[at * SUB : (at + 1) * SUB, :128], z[at * SUB : (at + 1) * SUB, 128:]
                halves.append(jnp.concatenate([re * cos + im * sin, im * cos - re * sin], 0))
            pairs.append(split(jnp.concatenate(halves, 1)))
        values = [dot(left[0], jnp.concatenate([high, low, high], 0)) for high, low in pairs]
        pairs = []
        for f in values:
            sr, si, fr, fi = f[:SUB, :128], f[SUB:, :128], f[:SUB, 128:], f[SUB:, 128:]
            pairs.append(split(jnp.concatenate([sr * fr - si * fi, sr * fi + si * fr], 0)))
        values = [dot(left[1], jnp.concatenate([high, low, high], 0)) for high, low in pairs]
        pairs = []
        for a, g in zip(several, values):
            cos, sin = turn[a, 0], turn[a, 1]
            re, im = g[:SUB], g[SUB:]
            pairs.append(split(jnp.concatenate([re * cos - im * sin, im * cos + re * sin], 1)))
        for a, (high, low) in zip(several, pairs):
            back[a] = dot(high, inv[0, a]) + dot(low, inv[0, a]) + dot(high, inv[1, a])
    for s in range(5):
        sums = {}
        for a in range(COARSE):
            cos, sin = math.cos(2 * math.pi * s * a / 16), math.sin(2 * math.pi * s * a / 16)
            for name, factor, lanes in (("c", cos, 0), ("s", sin, 128)):
                if abs(factor) > 1e-9:
                    term = back[a, :, lanes : lanes + 128] * np.float32(factor)
                    key = name + "eo"[a % 2]
                    sums[key] = sums[key] + term if key in sums else term
        zero = jnp.zeros((SUB, 128), F32)
        ce, co, se, so = (sums.get(key, zero) for key in ("ce", "co", "se", "so"))
        send_b[s] = (ce + co - se - so).astype(BF16)
        if s in (1, 2, 3):
            send_b[8 - s] = (ce - co + se - so).astype(BF16)

    copies_b = [
        remote(send_b.at[lax.rem(me_s + k, SEQ_DEV)], recv_b.at[me_s], sem_b, k, on_seq(k))
        for k in SEQ_ORDER
    ]
    recv_b[me_s] = send_b[me_s]
    finish(copies_v)
    for o in range(2):
        total = recv_v[o, 0].astype(F32)
        for n in range(1, NEAR):
            total = total + recv_v[o, n].astype(F32)
        v_near[me_s, o] = total.astype(BF16)
    copies_u = [
        remote(v_near.at[me_s], v_near.at[me_s], sem_u, k, on_seq(k)) for k in SEQ_ORDER
    ]
    finish(copies_w)
    copies_k = [
        remote(w_group.at[o, half], w_group.at[o, half], sem_k, o, other_core) for o in range(2)
    ]
    finish(in_gate, copies_b)
    own = [pl.ds(pl.multiple_of(member[o] * CHANS, CHANS), CHANS) for o in range(2)]
    others = [
        pl.ds(pl.multiple_of((member[o] + 1 - 2 * beside) * CHANS, CHANS), CHANS) for o in range(2)
    ]
    convolved = block_transpose([recv_b[d].astype(F32) for d in range(8)])
    copies_g, copies_m = [], []
    for i in range(CHUNKS):
        for q in range(i * 8 // CHUNKS, (i + 1) * 8 // CHUNKS):
            rows = slice(q * SUB, (q + 1) * SUB)
            value = convolved[q] + skip[...] * sig[rows, :].astype(F32)
            depth[rows, own[i % 2]] = (gat[rows, :].astype(F32) * value).astype(BF16)
        o, at = i % 2, i * NEAR
        block = depth.at[i * STEP : (i + 1) * STEP, own[o]]
        copies_m.append(remote(block, block, sem_g, at, other_line))
        copies_g.append([remote(block, block, sem_g, at + k, on_line(o, k)) for k in range(1, FAR)])
    for i in range(CHUNKS):
        o, at = i % 2, i * NEAR + FAR
        copies_m[i].wait()
        block = depth.at[i * STEP : (i + 1) * STEP, others[o]]
        copies_g[i] += [remote(block, block, sem_g, at + k, on_line(o, k)) for k in range(1, FAR)]

    copies_p, copies_q, copies_y = [], [], []

    def sum_y(i):
        finish(copies_q[i])
        total = part_y[i, 0]
        for f in range(1, FAR):
            total = total + part_y[i, f]
        o = i % 2
        near_y[i, member[o]] = total.astype(BF16)
        block = near_y.at[i, member[o]]
        copies_y.append(
            [remote(block, block, sem_y, i * NEAR + k, on_member(o, k)) for k in range(1, NEAR)]
        )

    finish(copies_k, copies_u)
    for i in range(CHUNKS):
        rows, o = slice(i * STEP, (i + 1) * STEP), i % 2
        finish(copies_g[i])
        block = depth[rows, :]
        product = jnp.concatenate([v_near[s, o] for s in range(SEQ_DEV)], 1)
        part_y[i, group[o]] = lax.dot_general(
            product, block, (((1,), (1,)), ((), ())), preferred_element_type=F32
        )
        sums = part_y.at[i, group[o]]
        copies_q.append([remote(sums, sums, sem_q, i * FAR + k, on_far(o, k)) for k in range(1, FAR)])
        projected = dot(block, w_group[o].reshape(NEAR * CHANS, FAR * CHANS))
        for f in range(FAR):
            part[f, rows, :] = projected[:, f * CHANS : (f + 1) * CHANS].astype(BF16)
        copies_p.append(
            [
                remote(
                    part.at[lax.rem(group[o] + k, FAR), rows, :], recv_p.at[group[o], rows, :],
                    sem_p, i * FAR + k, on_far(o, k),
                )
                for k in range(1, FAR)
            ]
        )
        recv_p[group[o], rows, :] = part[group[o], rows, :]
        if i:
            sum_y(i - 1)
    sum_y(CHUNKS - 1)
    for i in range(CHUNKS):
        rows = slice(i * STEP, (i + 1) * STEP)
        finish(copies_p[i])
        total = recv_p[0, rows, :].astype(F32)
        for f in range(1, FAR):
            total = total + recv_p[f, rows, :].astype(F32)
        mixed[rows, :] = total.astype(BF16)

    sum_z = jnp.zeros((RANK, CHANS), F32)
    for i in range(CHUNKS):
        finish(copies_y[i])
        sum_z = sum_z + dot(near_y[i].reshape(RANK, STEP), mixed[i * STEP : (i + 1) * STEP, :])
    part_z[...] = (sum_z * np.float32(1.0 / (SEQ_DEV * ROWS))).reshape(2, CHANS, CHANS)
    send_z[...] = part_z[1 - core].astype(BF16)
    copies_c = [remote(send_z, recv_z, sem_c, 0, other_core)]
    finish(copies_c)
    high = me_s // 2
    recv_h[high] = (part_z[core] + recv_z[...].astype(F32)).astype(BF16)
    copies_h = [remote(recv_h.at[high], recv_h.at[high], sem_h, k, on_seq(2 * k)) for k in (2, 1, 3)]
    for i in range(CHUNKS):
        out_y[i * STEP : (i + 1) * STEP, :] = near_y[i].reshape(RANK, STEP).astype(F32).T
    finish(copies_h)
    total = recv_h[0].astype(F32)
    for h in range(1, 4):
        total = total + recv_h[h].astype(F32)
    full_z[core] = total.astype(BF16)
    copies_f = [remote(full_z.at[core], full_z.at[core], sem_f, 0, other_core)]
    finish(copies_f)
    out_z[...] = full_z[...].reshape(RANK, CHANS).astype(F32).T


def store(*refs):
    ins, outs, held, sems = refs[:3], refs[3:6], refs[6:9], refs[9]
    first = [pltpu.make_async_copy(a, b, sems.at[0, k]) for k, (a, b) in enumerate(zip(ins, held))]
    second = [pltpu.make_async_copy(a, b, sems.at[1, k]) for k, (a, b) in enumerate(zip(held, outs))]
    for copy in first:
        copy.start()
    for k in range(3):
        first[k].wait()
        second[k].start()
    for copy in second:
        copy.wait()


def per_device(signal, gating, filter_taps, skip_bias, out_weight, test_matrix):
    vmem = pl.BlockSpec(memory_space=pltpu.VMEM)
    constants = [jnp.asarray(t) for t in tables()]
    weight = out_weight.reshape(FAR, FAR, 2 * CHANS, CHANS)
    args = [signal, gating, filter_taps, skip_bias[None, :], weight, test_matrix] + constants
    outs = (
        jax.ShapeDtypeStruct((ROWS, CHANS), BF16),
        jax.ShapeDtypeStruct((ROWS, RANK), F32),
        jax.ShapeDtypeStruct((CHANS, RANK), F32),
    )

    def sems(n):
        return pltpu.SemaphoreType.DMA((2, n))

    results = pl.pallas_call(
        kernel,
        out_shape=outs,
        in_specs=[pl.BlockSpec(memory_space=pl.ANY)] * len(args),
        out_specs=(vmem, vmem, vmem),
        scratch_shapes=[
            pltpu.VMEM((ROWS, CHANS), BF16),
            pltpu.VMEM((ROWS, CHANS), BF16),
            pltpu.VMEM((ROWS, CHANS), BF16),
            pltpu.VMEM((1, CHANS), F32),
        ]
        + [pltpu.VMEM(c.shape, c.dtype) for c in constants]
        + [
            pltpu.SemaphoreType.DMA((14,)),
            pltpu.VMEM((SEQ_DEV, 2 * SUB, 128), BF16),
            pltpu.VMEM((SEQ_DEV, 2 * SUB, 128), BF16),
            pltpu.VMEM((SEQ_DEV, SUB, 128), BF16),
            pltpu.VMEM((SEQ_DEV, SUB, 128), BF16),
            pltpu.VMEM((ROWS, NEAR * CHANS), BF16),
            pltpu.VMEM((2, FAR, 2 * CHANS, FAR * CHANS), BF16),
            pltpu.VMEM((FAR, ROWS, CHANS), BF16),
            pltpu.VMEM((FAR, ROWS, CHANS), BF16),
            pltpu.VMEM((COARSE, 2 * SUB, 256), F32),
            pltpu.VMEM((COARSE, SUB, 256), F32),
            pltpu.VMEM((2, FAR, CHANS, RANK), BF16),
            pltpu.VMEM((2, CHANS, FAR * CHANS), BF16),
            pltpu.VMEM((2, NEAR, SLICE, CHANS), BF16),
            pltpu.VMEM((2, NEAR, SLICE, CHANS), BF16),
            pltpu.VMEM((SEQ_DEV, 2, SLICE, CHANS), BF16),
            pltpu.VMEM((CHUNKS, FAR, SLICE, STEP), F32),
            pltpu.VMEM((CHUNKS, NEAR, SLICE, STEP), BF16),
            pltpu.VMEM((2, CHANS, CHANS), F32),
            pltpu.VMEM((CHANS, CHANS), BF16),
            pltpu.VMEM((CHANS, CHANS), BF16),
            pltpu.VMEM((4, CHANS, CHANS), BF16),
            pltpu.VMEM((2, CHANS, CHANS), BF16),
            sems(SEQ_DEV), sems(SEQ_DEV), sems(CHUNKS * NEAR), sems(2 * FAR), sems(2 * FAR),
            sems(2 * FAR), sems(2 * NEAR), sems(SEQ_DEV), sems(CHUNKS * FAR), sems(CHUNKS * FAR), sems(CHUNKS * NEAR),
            sems(1), sems(4), sems(1), sems(2),
        ],
        compiler_params=pltpu.CompilerParams(
            collective_id=0, has_side_effects=True, vmem_limit_bytes=60 * 2**20
        ),
    )(*args)
    return pl.pallas_call(
        store,
        out_shape=outs,
        in_specs=[pl.BlockSpec(memory_space=pl.ANY)] * 3,
        out_specs=(pl.BlockSpec(memory_space=pl.ANY),) * 3,
        scratch_shapes=[pltpu.VMEM(o.shape, o.dtype) for o in outs]
        + [pltpu.SemaphoreType.DMA((2, 3))],
        compiler_params=pltpu.CompilerParams(vmem_limit_bytes=60 * 2**20),
    )(*results)


def solution(mesh):
    return jax.shard_map(
        per_device,
        mesh=mesh,
        in_specs=(
            P("seq", "chan"), P("seq", "chan"), P("seq", "chan"),
            P("chan"), P(None, "chan"), P("chan", None),
        ),
        out_specs=(P("seq", "chan"), P("seq", None), P("chan", None)),
        check_vma=False,
    )
```

```python
import functools
import math

import jax
import jax.numpy as jnp
import numpy as np
from jax import lax
from jax.experimental import pallas as pl
from jax.experimental.pallas import tpu as pltpu
from jax.sharding import PartitionSpec as P

MESH = pl.DeviceIdType.MESH
F32, BF16 = jnp.float32, jnp.bfloat16

SEQ_DEV = 8
CHAN_DEV = 32
NEAR = 8
FAR = 4
ROWS = 512
CHANS = 128
SUB = 64
LANES = 16
COARSE = 9
RANK = 256
SLICE = RANK // NEAR
TOGETHER = 3
CHUNKS = 2
STEP = ROWS // CHUNKS
SEQ_ORDER = (4, 3, 5, 2, 6, 1, 7)


def split_np(x):
    high = x.astype(jnp.bfloat16)
    low = (x - high.astype(np.float64)).astype(jnp.bfloat16)
    return high, low


@functools.lru_cache(None)
def tables():
    n = 2 * SEQ_DEV * ROWS
    j = np.arange(SUB)
    q = np.arange(8)
    b = np.arange(8)
    turn = []
    fwd, inv = [], []
    eye = np.eye(LANES)
    for a in range(COARSE):
        k1 = a + 16 * b
        angle = 2 * np.pi * np.outer(j, k1) / n
        turn.append((np.repeat(np.cos(angle), LANES, 1), np.repeat(np.sin(angle), LANES, 1)))
        ang = 2 * np.pi * np.outer(q, k1) / 128
        c, s = np.kron(np.cos(ang), eye), np.kron(np.sin(ang), eye)
        fwd.append(np.block([[c, -s], [s, c]]))
        weight = (1.0 if a in (0, 8) else 2.0) / n
        inv.append(np.block([[c.T, s.T], [-s.T, c.T]]) * weight)
    fine = 2 * np.pi * np.outer(j, j) / SUB
    c, s = np.cos(fine), np.sin(fine)
    left = np.block([[c, s], [-s, c]])
    left_inv = np.block([[c, -s], [s, c]])

    def triple(m):
        high, low = split_np(m)
        return np.concatenate([high, high, low], 1)

    fwd = np.stack(split_np(np.stack(fwd)))
    inv = np.stack(split_np(np.stack(inv)))
    turn = np.stack([np.stack(t) for t in turn]).astype(np.float32)
    return turn, np.stack([triple(left), triple(left_inv)]), fwd, inv


def dot(a, b):
    return lax.dot_general(a, b, (((1,), (0,)), ((), ())), preferred_element_type=F32)


def split(x):
    high = x.astype(BF16)
    return high, (x - high.astype(F32)).astype(BF16)


def block_transpose(blocks):
    lane = lax.broadcasted_iota(jnp.int32, (SUB, 128), 1)
    for bit in range(3):
        step = LANES << bit
        low = (lane & step) == 0
        new = list(blocks)
        for q in range(8):
            if q >> bit & 1:
                continue
            p = q | 1 << bit
            new[q] = jnp.where(low, blocks[q], pltpu.roll(blocks[p], step, 1))
            new[p] = jnp.where(low, pltpu.roll(blocks[q], 128 - step, 1), blocks[p])
        blocks = new
    return blocks


def coarse_forward(x):
    plus = {s: x[s] + x[8 - s] for s in (1, 2, 3)}
    minus = {s: x[s] - x[8 - s] for s in (1, 2, 3)}

    def total(terms):
        out = None
        for factor, value in terms:
            if abs(factor) < 1e-9:
                continue
            if abs(factor - 1) < 1e-9:
                term = value
            elif abs(factor + 1) < 1e-9:
                term = -value
            else:
                term = value * np.float32(factor)
            out = term if out is None else out + term
        return jnp.zeros_like(x[0]) if out is None else out

    result = []
    for a in range(COARSE):
        cos = lambda s: math.cos(2 * math.pi * s * a / 16)
        sin = lambda s: math.sin(2 * math.pi * s * a / 16)
        even, odd = (plus, minus) if a % 2 == 0 else (minus, plus)
        re = total([(1.0, x[0]), (cos(4), x[4])] + [(cos(s), even[s]) for s in (1, 2, 3)])
        im = total([(-sin(4), x[4])] + [(-sin(s), odd[s]) for s in (1, 2, 3)])
        result.append((re, im))
    return result


def kernel(
    sig_in, gat_in, fil_in, skip_in, w, test_in, turn_in, left_in, fwd_in, inv_in,
    to_mixed, to_y, to_z,
    mixed, out_y, out_z,
    sig, gat, fil, skip, turn, left, fwd, inv, sem_in,
    send_a, recv_a, send_b, recv_b, depth, w_group, part, recv_p, spec, back,
    test, w_rows, send_v, recv_v, v_near, part_y, near_y,
    part_z, send_z, recv_z, recv_h, full_z,
    sem_a, sem_b, sem_g, sem_w, sem_r, sem_e, sem_v, sem_u, sem_p, sem_q, sem_y, sem_c, sem_h, sem_f, sem_k,
):
    me_s, me_c = lax.axis_index("seq"), lax.axis_index("chan")
    core = me_s % 2
    place = ((me_c // 2) % FAR, me_c // NEAR)
    beside = me_c % 2
    group = (place[1], place[0])
    member = (2 * place[0] + beside, 2 * place[1] + beside)

    def on_seq(k):
        return {"seq": lax.rem(me_s + k, SEQ_DEV), "chan": me_c}

    def on_line(o, k):
        at = lax.rem(place[o] + k, FAR)
        chan = NEAR * place[1] + 2 * at + beside if o == 0 else NEAR * at + 2 * place[0] + beside
        return {"seq": me_s, "chan": chan}

    def on_far(o, k):
        return on_line(1 - o, k)

    def on_member(o, k):
        at = lax.rem(member[o] + k, NEAR)
        chan = NEAR * place[1] + at if o == 0 else NEAR * (at // 2) + 2 * place[0] + at % 2
        return {"seq": me_s, "chan": chan}

    other_line = {"seq": me_s, "chan": me_c + 1 - 2 * beside}
    other_core = {"seq": me_s + 1 - 2 * core, "chan": me_c}

    sending = []

    def remote(src, dst, sems, k, target):
        copy = pltpu.make_async_remote_copy(
            src_ref=src, dst_ref=dst, send_sem=sems.at[0, k], recv_sem=sems.at[1, k],
            device_id=target, device_id_type=MESH,
        )
        copy.start()
        sending.append(copy)
        return copy

    def local(k, src, dst):
        copy = pltpu.make_async_copy(src, dst, sem_in.at[k])
        copy.start()
        return copy

    def finish(*groups):
        for copies in groups:
            for copy in copies:
                if copy.is_remote:
                    copy.wait_recv()
                else:
                    copy.wait()

    def settle():
        for copy in sending:
            copy.wait_send()
        sending.clear()

    in_sig = [local(0, sig_in, sig), local(1, fil_in, fil)]
    in_tables = [
        local(2, fwd_in, fwd), local(3, turn_in, turn), local(4, left_in, left), local(5, inv_in, inv)
    ]
    in_gate = [local(6, gat_in, gat), local(7, skip_in, skip)]

    barrier = pltpu.get_barrier_semaphore()
    for k in range(1, SEQ_DEV):
        pl.semaphore_signal(barrier, inc=1, device_id=on_seq(k), device_id_type=MESH)
    for o in range(2):
        for k in range(1, NEAR):
            pl.semaphore_signal(barrier, inc=1, device_id=on_member(o, k), device_id_type=MESH)

    finish(in_sig)
    for at, source in enumerate((sig, fil)):
        blocks = [source[q * SUB : (q + 1) * SUB, :].astype(F32) for q in range(8)]
        for d, block in enumerate(block_transpose(blocks)):
            send_a[d, at * SUB : (at + 1) * SUB, :] = block.astype(BF16)

    pl.semaphore_wait(barrier, SEQ_DEV - 1 + 2 * (NEAR - 1))

    copies_a = [
        remote(send_a.at[lax.rem(me_s + k, SEQ_DEV)], recv_a.at[me_s], sem_a, k, on_seq(k))
        for k in SEQ_ORDER
    ]

    copies_e, copies_r, copies_w = [], [], []

    def weight(o, target, part, count):
        return w.at[target, pl.ds(part, count)] if o == 0 else w.at[pl.ds(part, count), target]

    def weight_rows(o, target):
        rows = pl.ds(pl.multiple_of(core * CHANS, CHANS), CHANS)
        return w.at[target, me_s // 2, rows] if o == 0 else w.at[me_s // 2, target, rows]

    columns = [pl.ds(pl.multiple_of(group[o] * CHANS, CHANS), CHANS) for o in range(2)]
    for o in range(2):
        for k in range(1, FAR):
            rows = weight_rows(o, lax.rem(group[o] + k, FAR))
            copies_r.append(
                remote(rows, w_rows.at[o, :, columns[o]], sem_r, o * FAR + k, on_far(o, k))
            )
            copies_e.append(remote(test_in, test.at[o, group[o]], sem_e, o * FAR + k, on_far(o, k)))
        copies_r.append(local(8 + o, weight_rows(o, group[o]), w_rows.at[o, :, columns[o]]))
        copies_e.append(local(10 + o, test_in, test.at[o, group[o]]))
    half = pl.ds(2 * core, 2)
    for o in range(2):
        target = w_group.at[o, half, :, columns[o]]
        for k in range(1, FAR):
            rows = weight(o, lax.rem(group[o] + k, FAR), 2 * core, 2)
            copies_w.append(remote(rows, target, sem_w, o * FAR + k, on_far(o, k)))
        copies_w.append(local(12 + o, weight(o, group[o], 2 * core, 2), target))
    recv_a[me_s] = send_a[me_s]

    finish(copies_r, copies_e)
    for o in range(2):
        product = jnp.zeros((CHANS, RANK), F32)
        for f in range(FAR):
            product = product + dot(w_rows[o, :, f * CHANS : (f + 1) * CHANS], test[o, f])
        send_v[o] = product.T.reshape(NEAR, SLICE, CHANS).astype(BF16)

    finish(copies_a)
    copies_v = []
    for o in range(2):
        for k in range(1, NEAR):
            block = send_v.at[o, lax.rem(member[o] + k, NEAR)]
            copies_v.append(
                remote(block, recv_v.at[o, member[o]], sem_v, o * NEAR + k, on_member(o, k))
            )
        recv_v[o, member[o]] = send_v[o, member[o]]
    finish(in_tables)
    for at in range(2):
        blocks = [recv_a[s, at * SUB : (at + 1) * SUB, :].astype(F32) for s in range(SEQ_DEV)]
        for a, (re, im) in enumerate(coarse_forward(blocks)):
            spec[a, at * SUB : (at + 1) * SUB, :128] = re
            spec[a, at * SUB : (at + 1) * SUB, 128:] = im
    for first in range(0, COARSE, TOGETHER):
        several = range(first, min(first + TOGETHER, COARSE))
        pairs = [split(spec[a]) for a in several]
        values = [
            dot(high, fwd[0, a]) + dot(low, fwd[0, a]) + dot(high, fwd[1, a])
            for a, (high, low) in zip(several, pairs)
        ]
        pairs = []
        for a, z in zip(several, values):
            cos, sin = turn[a, 0], turn[a, 1]
            halves = []
            for at in range(2):
                re, im = z[at * SUB : (at + 1) * SUB, :128], z[at * SUB : (at + 1) * SUB, 128:]
                halves.append(jnp.concatenate([re * cos + im * sin, im * cos - re * sin], 0))
            pairs.append(split(jnp.concatenate(halves, 1)))
        values = [dot(left[0], jnp.concatenate([high, low, high], 0)) for high, low in pairs]
        pairs = []
        for f in values:
            sr, si, fr, fi = f[:SUB, :128], f[SUB:, :128], f[:SUB, 128:], f[SUB:, 128:]
            pairs.append(split(jnp.concatenate([sr * fr - si * fi, sr * fi + si * fr], 0)))
        values = [dot(left[1], jnp.concatenate([high, low, high], 0)) for high, low in pairs]
        pairs = []
        for a, g in zip(several, values):
            cos, sin = turn[a, 0], turn[a, 1]
            re, im = g[:SUB], g[SUB:]
            pairs.append(split(jnp.concatenate([re * cos - im * sin, im * cos + re * sin], 1)))
        for a, (high, low) in zip(several, pairs):
            back[a] = dot(high, inv[0, a]) + dot(low, inv[0, a]) + dot(high, inv[1, a])
    for s in range(5):
        sums = {}
        for a in range(COARSE):
            cos, sin = math.cos(2 * math.pi * s * a / 16), math.sin(2 * math.pi * s * a / 16)
            for name, factor, lanes in (("c", cos, 0), ("s", sin, 128)):
                if abs(factor) > 1e-9:
                    term = back[a, :, lanes : lanes + 128] * np.float32(factor)
                    key = name + "eo"[a % 2]
                    sums[key] = sums[key] + term if key in sums else term
        zero = jnp.zeros((SUB, 128), F32)
        ce, co, se, so = (sums.get(key, zero) for key in ("ce", "co", "se", "so"))
        send_b[s] = (ce + co - se - so).astype(BF16)
        if s in (1, 2, 3):
            send_b[8 - s] = (ce - co + se - so).astype(BF16)

    copies_b = [
        remote(send_b.at[lax.rem(me_s + k, SEQ_DEV)], recv_b.at[me_s], sem_b, k, on_seq(k))
        for k in SEQ_ORDER
    ]
    recv_b[me_s] = send_b[me_s]
    finish(copies_v)
    for o in range(2):
        total = recv_v[o, 0].astype(F32)
        for n in range(1, NEAR):
            total = total + recv_v[o, n].astype(F32)
        v_near[me_s, o] = total.astype(BF16)
    copies_u = [
        remote(v_near.at[me_s], v_near.at[me_s], sem_u, k, on_seq(k)) for k in SEQ_ORDER
    ]
    finish(copies_w)
    copies_k = [
        remote(w_group.at[o, half], w_group.at[o, half], sem_k, o, other_core) for o in range(2)
    ]
    finish(in_gate, copies_b)
    own = [pl.ds(pl.multiple_of(member[o] * CHANS, CHANS), CHANS) for o in range(2)]
    others = [
        pl.ds(pl.multiple_of((member[o] + 1 - 2 * beside) * CHANS, CHANS), CHANS) for o in range(2)
    ]
    convolved = block_transpose([recv_b[d].astype(F32) for d in range(8)])
    copies_g, copies_m = [], []
    for i in range(CHUNKS):
        for q in range(i * 8 // CHUNKS, (i + 1) * 8 // CHUNKS):
            rows = slice(q * SUB, (q + 1) * SUB)
            value = convolved[q] + skip[...] * sig[rows, :].astype(F32)
            depth[rows, own[i % 2]] = (gat[rows, :].astype(F32) * value).astype(BF16)
        o, at = i % 2, i * NEAR
        block = depth.at[i * STEP : (i + 1) * STEP, own[o]]
        copies_m.append(remote(block, block, sem_g, at, other_line))
        copies_g.append([remote(block, block, sem_g, at + k, on_line(o, k)) for k in range(1, FAR)])
    for i in range(CHUNKS):
        o, at = i % 2, i * NEAR + FAR
        copies_m[i].wait_recv()
        block = depth.at[i * STEP : (i + 1) * STEP, others[o]]
        copies_g[i] += [remote(block, block, sem_g, at + k, on_line(o, k)) for k in range(1, FAR)]

    copies_p, copies_q, copies_y = [], [], []

    def sum_y(i):
        finish(copies_q[i])
        total = part_y[i, 0]
        for f in range(1, FAR):
            total = total + part_y[i, f]
        o = i % 2
        near_y[i, member[o]] = total.astype(BF16)
        block = near_y.at[i, member[o]]
        copies_y.append(
            [remote(block, block, sem_y, i * NEAR + k, on_member(o, k)) for k in range(1, NEAR)]
        )

    finish(copies_k, copies_u)
    for i in range(CHUNKS):
        rows, o = slice(i * STEP, (i + 1) * STEP), i % 2
        finish(copies_g[i])
        block = depth[rows, :]
        product = jnp.concatenate([v_near[s, o] for s in range(SEQ_DEV)], 1)
        part_y[i, group[o]] = lax.dot_general(
            product, block, (((1,), (1,)), ((), ())), preferred_element_type=F32
        )
        sums = part_y.at[i, group[o]]
        copies_q.append([remote(sums, sums, sem_q, i * FAR + k, on_far(o, k)) for k in range(1, FAR)])
    for i in range(CHUNKS):
        rows, o = slice(i * STEP, (i + 1) * STEP), i % 2
        projected = dot(depth[rows, :], w_group[o].reshape(NEAR * CHANS, FAR * CHANS))
        for f in range(FAR):
            part[f, rows, :] = projected[:, f * CHANS : (f + 1) * CHANS].astype(BF16)
        copies_p.append(
            [
                remote(
                    part.at[lax.rem(group[o] + k, FAR), rows, :], recv_p.at[group[o], rows, :],
                    sem_p, i * FAR + k, on_far(o, k),
                )
                for k in range(1, FAR)
            ]
        )
        recv_p[group[o], rows, :] = part[group[o], rows, :]
    for i in range(CHUNKS):
        sum_y(i)
    for i in range(CHUNKS):
        rows = slice(i * STEP, (i + 1) * STEP)
        finish(copies_p[i])
        total = recv_p[0, rows, :].astype(F32)
        for f in range(1, FAR):
            total = total + recv_p[f, rows, :].astype(F32)
        mixed[rows, :] = total.astype(BF16)
    stores = [local(14, mixed, to_mixed)]

    sum_z = jnp.zeros((RANK, CHANS), F32)
    for i in range(CHUNKS):
        finish(copies_y[i])
        sum_z = sum_z + dot(near_y[i].reshape(RANK, STEP), mixed[i * STEP : (i + 1) * STEP, :])
    part_z[...] = (sum_z * np.float32(1.0 / (SEQ_DEV * ROWS))).reshape(2, CHANS, CHANS)
    send_z[...] = part_z[1 - core].astype(BF16)
    copies_c = [remote(send_z, recv_z, sem_c, 0, other_core)]
    finish(copies_c)
    high = me_s // 2
    recv_h[high] = (part_z[core] + recv_z[...].astype(F32)).astype(BF16)
    copies_h = [remote(recv_h.at[high], recv_h.at[high], sem_h, k, on_seq(2 * k)) for k in (2, 1, 3)]
    for i in range(CHUNKS):
        out_y[i * STEP : (i + 1) * STEP, :] = near_y[i].reshape(RANK, STEP).astype(F32).T
    stores.append(local(15, out_y, to_y))
    settle()
    finish(copies_h)
    total = recv_h[0].astype(F32)
    for h in range(1, 4):
        total = total + recv_h[h].astype(F32)
    full_z[core] = total.astype(BF16)
    copies_f = [remote(full_z.at[core], full_z.at[core], sem_f, 0, other_core)]
    finish(copies_f)
    out_z[...] = full_z[...].reshape(RANK, CHANS).astype(F32).T
    stores.append(local(16, out_z, to_z))
    settle()
    finish(stores)


def store(*refs):
    ins, outs, held, sems = refs[:3], refs[3:6], refs[6:9], refs[9]
    first = [pltpu.make_async_copy(a, b, sems.at[0, k]) for k, (a, b) in enumerate(zip(ins, held))]
    second = [pltpu.make_async_copy(a, b, sems.at[1, k]) for k, (a, b) in enumerate(zip(held, outs))]
    for copy in first:
        copy.start()
    for k in range(3):
        first[k].wait()
        second[k].start()
    for copy in second:
        copy.wait()


def per_device(signal, gating, filter_taps, skip_bias, out_weight, test_matrix):
    constants = [jnp.asarray(t) for t in tables()]
    weight = out_weight.reshape(FAR, FAR, 2 * CHANS, CHANS)
    args = [signal, gating, filter_taps, skip_bias[None, :], weight, test_matrix] + constants
    outs = (
        jax.ShapeDtypeStruct((ROWS, CHANS), BF16),
        jax.ShapeDtypeStruct((ROWS, RANK), F32),
        jax.ShapeDtypeStruct((CHANS, RANK), F32),
    )

    def sems(n):
        return pltpu.SemaphoreType.DMA((2, n))

    results = pl.pallas_call(
        kernel,
        out_shape=outs,
        in_specs=[pl.BlockSpec(memory_space=pl.ANY)] * len(args),
        out_specs=(pl.BlockSpec(memory_space=pl.ANY),) * 3,
        scratch_shapes=[pltpu.VMEM(o.shape, o.dtype) for o in outs]
        + [
            pltpu.VMEM((ROWS, CHANS), BF16),
            pltpu.VMEM((ROWS, CHANS), BF16),
            pltpu.VMEM((ROWS, CHANS), BF16),
            pltpu.VMEM((1, CHANS), F32),
        ]
        + [pltpu.VMEM(c.shape, c.dtype) for c in constants]
        + [
            pltpu.SemaphoreType.DMA((17,)),
            pltpu.VMEM((SEQ_DEV, 2 * SUB, 128), BF16),
            pltpu.VMEM((SEQ_DEV, 2 * SUB, 128), BF16),
            pltpu.VMEM((SEQ_DEV, SUB, 128), BF16),
            pltpu.VMEM((SEQ_DEV, SUB, 128), BF16),
            pltpu.VMEM((ROWS, NEAR * CHANS), BF16),
            pltpu.VMEM((2, FAR, 2 * CHANS, FAR * CHANS), BF16),
            pltpu.VMEM((FAR, ROWS, CHANS), BF16),
            pltpu.VMEM((FAR, ROWS, CHANS), BF16),
            pltpu.VMEM((COARSE, 2 * SUB, 256), F32),
            pltpu.VMEM((COARSE, SUB, 256), F32),
            pltpu.VMEM((2, FAR, CHANS, RANK), BF16),
            pltpu.VMEM((2, CHANS, FAR * CHANS), BF16),
            pltpu.VMEM((2, NEAR, SLICE, CHANS), BF16),
            pltpu.VMEM((2, NEAR, SLICE, CHANS), BF16),
            pltpu.VMEM((SEQ_DEV, 2, SLICE, CHANS), BF16),
            pltpu.VMEM((CHUNKS, FAR, SLICE, STEP), F32),
            pltpu.VMEM((CHUNKS, NEAR, SLICE, STEP), BF16),
            pltpu.VMEM((2, CHANS, CHANS), F32),
            pltpu.VMEM((CHANS, CHANS), BF16),
            pltpu.VMEM((CHANS, CHANS), BF16),
            pltpu.VMEM((4, CHANS, CHANS), BF16),
            pltpu.VMEM((2, CHANS, CHANS), BF16),
            sems(SEQ_DEV), sems(SEQ_DEV), sems(CHUNKS * NEAR), sems(2 * FAR), sems(2 * FAR),
            sems(2 * FAR), sems(2 * NEAR), sems(SEQ_DEV), sems(CHUNKS * FAR), sems(CHUNKS * FAR), sems(CHUNKS * NEAR),
            sems(1), sems(4), sems(1), sems(2),
        ],
        compiler_params=pltpu.CompilerParams(
            collective_id=0, has_side_effects=True, vmem_limit_bytes=60 * 2**20
        ),
    )(*args)
    return pl.pallas_call(
        store,
        out_shape=outs,
        in_specs=[pl.BlockSpec(memory_space=pl.ANY)] * 3,
        out_specs=(pl.BlockSpec(memory_space=pl.ANY),) * 3,
        scratch_shapes=[pltpu.VMEM(o.shape, o.dtype) for o in outs]
        + [pltpu.SemaphoreType.DMA((2, 3))],
        compiler_params=pltpu.CompilerParams(vmem_limit_bytes=60 * 2**20),
    )(*results)


def solution(mesh):
    return jax.shard_map(
        per_device,
        mesh=mesh,
        in_specs=(
            P("seq", "chan"), P("seq", "chan"), P("seq", "chan"),
            P("chan"), P(None, "chan"), P("chan", None),
        ),
        out_specs=(P("seq", "chan"), P("seq", None), P("chan", None)),
        check_vma=False,
    )
```

```python
import functools
import math

import jax
import jax.numpy as jnp
import numpy as np
from jax import lax
from jax.experimental import pallas as pl
from jax.experimental.pallas import tpu as pltpu
from jax.sharding import PartitionSpec as P

MESH = pl.DeviceIdType.MESH
F32, BF16 = jnp.float32, jnp.bfloat16

SEQ_DEV = 8
CHAN_DEV = 32
NEAR = 8
FAR = 4
ROWS = 512
CHANS = 128
SUB = 64
LANES = 16
COARSE = 9
RANK = 256
SLICE = RANK // NEAR
TOGETHER = 3
CHUNKS = 4
STEP = ROWS // CHUNKS
SEQ_ORDER = (4, 3, 5, 2, 6, 1, 7)


def split_np(x):
    high = x.astype(jnp.bfloat16)
    low = (x - high.astype(np.float64)).astype(jnp.bfloat16)
    return high, low


@functools.lru_cache(None)
def tables():
    n = 2 * SEQ_DEV * ROWS
    j = np.arange(SUB)
    q = np.arange(8)
    b = np.arange(8)
    turn = []
    fwd, inv = [], []
    eye = np.eye(LANES)
    for a in range(COARSE):
        k1 = a + 16 * b
        angle = 2 * np.pi * np.outer(j, k1) / n
        turn.append((np.repeat(np.cos(angle), LANES, 1), np.repeat(np.sin(angle), LANES, 1)))
        ang = 2 * np.pi * np.outer(q, k1) / 128
        c, s = np.kron(np.cos(ang), eye), np.kron(np.sin(ang), eye)
        fwd.append(np.block([[c, -s], [s, c]]))
        weight = (1.0 if a in (0, 8) else 2.0) / n
        inv.append(np.block([[c.T, s.T], [-s.T, c.T]]) * weight)
    fine = 2 * np.pi * np.outer(j, j) / SUB
    c, s = np.cos(fine), np.sin(fine)
    left = np.block([[c, s], [-s, c]])
    left_inv = np.block([[c, -s], [s, c]])

    def triple(m):
        high, low = split_np(m)
        return np.concatenate([high, high, low], 1)

    fwd = np.stack(split_np(np.stack(fwd)))
    inv = np.stack(split_np(np.stack(inv)))
    turn = np.stack([np.stack(t) for t in turn]).astype(np.float32)
    return turn, np.stack([triple(left), triple(left_inv)]), fwd, inv


def dot(a, b):
    return lax.dot_general(a, b, (((1,), (0,)), ((), ())), preferred_element_type=F32)


def split(x):
    high = x.astype(BF16)
    return high, (x - high.astype(F32)).astype(BF16)


def block_transpose(blocks):
    lane = lax.broadcasted_iota(jnp.int32, (SUB, 128), 1)
    for bit in range(3):
        step = LANES << bit
        low = (lane & step) == 0
        new = list(blocks)
        for q in range(8):
            if q >> bit & 1:
                continue
            p = q | 1 << bit
            new[q] = jnp.where(low, blocks[q], pltpu.roll(blocks[p], step, 1))
            new[p] = jnp.where(low, pltpu.roll(blocks[q], 128 - step, 1), blocks[p])
        blocks = new
    return blocks


def coarse_forward(x):
    plus = {s: x[s] + x[8 - s] for s in (1, 2, 3)}
    minus = {s: x[s] - x[8 - s] for s in (1, 2, 3)}

    def total(terms):
        out = None
        for factor, value in terms:
            if abs(factor) < 1e-9:
                continue
            if abs(factor - 1) < 1e-9:
                term = value
            elif abs(factor + 1) < 1e-9:
                term = -value
            else:
                term = value * np.float32(factor)
            out = term if out is None else out + term
        return jnp.zeros_like(x[0]) if out is None else out

    result = []
    for a in range(COARSE):
        cos = lambda s: math.cos(2 * math.pi * s * a / 16)
        sin = lambda s: math.sin(2 * math.pi * s * a / 16)
        even, odd = (plus, minus) if a % 2 == 0 else (minus, plus)
        re = total([(1.0, x[0]), (cos(4), x[4])] + [(cos(s), even[s]) for s in (1, 2, 3)])
        im = total([(-sin(4), x[4])] + [(-sin(s), odd[s]) for s in (1, 2, 3)])
        result.append((re, im))
    return result


def kernel(
    sig_in, gat_in, fil_in, skip_in, w, test_in, turn_in, left_in, fwd_in, inv_in,
    to_mixed, to_y, to_z,
    mixed, out_y, out_z,
    sig, gat, fil, skip, turn, left, fwd, inv, sem_in,
    send_a, recv_a, send_b, recv_b, depth, w_group, part, recv_p, spec, back,
    test, w_rows, send_v, recv_v, v_near, part_y, near_y,
    part_z, send_z, recv_z, recv_h, full_z,
    sem_a, sem_b, sem_g, sem_w, sem_r, sem_e, sem_v, sem_u, sem_p, sem_q, sem_y, sem_c, sem_h, sem_f, sem_k,
):
    me_s, me_c = lax.axis_index("seq"), lax.axis_index("chan")
    core = me_s % 2
    place = ((me_c // 2) % FAR, me_c // NEAR)
    beside = me_c % 2
    group = (place[1], place[0])
    member = (2 * place[0] + beside, 2 * place[1] + beside)

    def on_seq(k):
        return {"seq": lax.rem(me_s + k, SEQ_DEV), "chan": me_c}

    def on_line(o, k):
        at = lax.rem(place[o] + k, FAR)
        chan = NEAR * place[1] + 2 * at + beside if o == 0 else NEAR * at + 2 * place[0] + beside
        return {"seq": me_s, "chan": chan}

    def on_far(o, k):
        return on_line(1 - o, k)

    def on_member(o, k):
        at = lax.rem(member[o] + k, NEAR)
        chan = NEAR * place[1] + at if o == 0 else NEAR * (at // 2) + 2 * place[0] + at % 2
        return {"seq": me_s, "chan": chan}

    other_line = {"seq": me_s, "chan": me_c + 1 - 2 * beside}
    other_core = {"seq": me_s + 1 - 2 * core, "chan": me_c}

    sending = []

    def remote(src, dst, sems, k, target):
        copy = pltpu.make_async_remote_copy(
            src_ref=src, dst_ref=dst, send_sem=sems.at[0, k], recv_sem=sems.at[1, k],
            device_id=target, device_id_type=MESH,
        )
        copy.start()
        sending.append(copy)
        return copy

    def local(k, src, dst):
        copy = pltpu.make_async_copy(src, dst, sem_in.at[k])
        copy.start()
        return copy

    def finish(*groups):
        for copies in groups:
            for copy in copies:
                if copy.is_remote:
                    copy.wait_recv()
                else:
                    copy.wait()

    def settle():
        for copy in sending:
            copy.wait_send()
        sending.clear()

    in_sig = [local(0, sig_in, sig), local(1, fil_in, fil)]
    in_tables = [
        local(2, fwd_in, fwd), local(3, turn_in, turn), local(4, left_in, left), local(5, inv_in, inv)
    ]
    in_gate = [local(6, gat_in, gat), local(7, skip_in, skip)]

    barrier = pltpu.get_barrier_semaphore()
    for k in range(1, SEQ_DEV):
        pl.semaphore_signal(barrier, inc=1, device_id=on_seq(k), device_id_type=MESH)
    for o in range(2):
        for k in range(1, NEAR):
            pl.semaphore_signal(barrier, inc=1, device_id=on_member(o, k), device_id_type=MESH)

    finish(in_sig)
    for at, source in enumerate((sig, fil)):
        blocks = [source[q * SUB : (q + 1) * SUB, :].astype(F32) for q in range(8)]
        for d, block in enumerate(block_transpose(blocks)):
            send_a[d, at * SUB : (at + 1) * SUB, :] = block.astype(BF16)

    pl.semaphore_wait(barrier, SEQ_DEV - 1 + 2 * (NEAR - 1))

    copies_a = [
        remote(send_a.at[lax.rem(me_s + k, SEQ_DEV)], recv_a.at[me_s], sem_a, k, on_seq(k))
        for k in SEQ_ORDER
    ]

    copies_e, copies_r, copies_w = [], [], []

    def weight(o, target, part, count):
        return w.at[target, pl.ds(part, count)] if o == 0 else w.at[pl.ds(part, count), target]

    def weight_rows(o, target):
        rows = pl.ds(pl.multiple_of(core * CHANS, CHANS), CHANS)
        return w.at[target, me_s // 2, rows] if o == 0 else w.at[me_s // 2, target, rows]

    columns = [pl.ds(pl.multiple_of(group[o] * CHANS, CHANS), CHANS) for o in range(2)]
    for o in range(2):
        for k in range(1, FAR):
            rows = weight_rows(o, lax.rem(group[o] + k, FAR))
            copies_r.append(
                remote(rows, w_rows.at[o, :, columns[o]], sem_r, o * FAR + k, on_far(o, k))
            )
            copies_e.append(remote(test_in, test.at[o, group[o]], sem_e, o * FAR + k, on_far(o, k)))
        copies_r.append(local(8 + o, weight_rows(o, group[o]), w_rows.at[o, :, columns[o]]))
        copies_e.append(local(10 + o, test_in, test.at[o, group[o]]))
    half = pl.ds(2 * core, 2)
    for o in range(2):
        target = w_group.at[o, half, :, columns[o]]
        for k in range(1, FAR):
            rows = weight(o, lax.rem(group[o] + k, FAR), 2 * core, 2)
            copies_w.append(remote(rows, target, sem_w, o * FAR + k, on_far(o, k)))
        copies_w.append(local(12 + o, weight(o, group[o], 2 * core, 2), target))
    recv_a[me_s] = send_a[me_s]

    finish(copies_r, copies_e)
    for o in range(2):
        product = jnp.zeros((CHANS, RANK), F32)
        for f in range(FAR):
            product = product + dot(w_rows[o, :, f * CHANS : (f + 1) * CHANS], test[o, f])
        send_v[o] = product.T.reshape(NEAR, SLICE, CHANS).astype(BF16)

    finish(copies_a)
    copies_v = []
    for o in range(2):
        for k in range(1, NEAR):
            block = send_v.at[o, lax.rem(member[o] + k, NEAR)]
            copies_v.append(
                remote(block, recv_v.at[o, member[o]], sem_v, o * NEAR + k, on_member(o, k))
            )
        recv_v[o, member[o]] = send_v[o, member[o]]
    finish(in_tables)
    for at in range(2):
        blocks = [recv_a[s, at * SUB : (at + 1) * SUB, :].astype(F32) for s in range(SEQ_DEV)]
        for a, (re, im) in enumerate(coarse_forward(blocks)):
            spec[a, at * SUB : (at + 1) * SUB, :128] = re
            spec[a, at * SUB : (at + 1) * SUB, 128:] = im
    for first in range(0, COARSE, TOGETHER):
        several = range(first, min(first + TOGETHER, COARSE))
        pairs = [split(spec[a]) for a in several]
        values = [
            dot(high, fwd[0, a]) + dot(low, fwd[0, a]) + dot(high, fwd[1, a])
            for a, (high, low) in zip(several, pairs)
        ]
        pairs = []
        for a, z in zip(several, values):
            cos, sin = turn[a, 0], turn[a, 1]
            halves = []
            for at in range(2):
                re, im = z[at * SUB : (at + 1) * SUB, :128], z[at * SUB : (at + 1) * SUB, 128:]
                halves.append(jnp.concatenate([re * cos + im * sin, im * cos - re * sin], 0))
            pairs.append(split(jnp.concatenate(halves, 1)))
        values = [dot(left[0], jnp.concatenate([high, low, high], 0)) for high, low in pairs]
        pairs = []
        for f in values:
            sr, si, fr, fi = f[:SUB, :128], f[SUB:, :128], f[:SUB, 128:], f[SUB:, 128:]
            pairs.append(split(jnp.concatenate([sr * fr - si * fi, sr * fi + si * fr], 0)))
        values = [dot(left[1], jnp.concatenate([high, low, high], 0)) for high, low in pairs]
        pairs = []
        for a, g in zip(several, values):
            cos, sin = turn[a, 0], turn[a, 1]
            re, im = g[:SUB], g[SUB:]
            pairs.append(split(jnp.concatenate([re * cos - im * sin, im * cos + re * sin], 1)))
        for a, (high, low) in zip(several, pairs):
            back[a] = dot(high, inv[0, a]) + dot(low, inv[0, a]) + dot(high, inv[1, a])
    for s in range(5):
        sums = {}
        for a in range(COARSE):
            cos, sin = math.cos(2 * math.pi * s * a / 16), math.sin(2 * math.pi * s * a / 16)
            for name, factor, lanes in (("c", cos, 0), ("s", sin, 128)):
                if abs(factor) > 1e-9:
                    term = back[a, :, lanes : lanes + 128] * np.float32(factor)
                    key = name + "eo"[a % 2]
                    sums[key] = sums[key] + term if key in sums else term
        zero = jnp.zeros((SUB, 128), F32)
        ce, co, se, so = (sums.get(key, zero) for key in ("ce", "co", "se", "so"))
        send_b[s] = (ce + co - se - so).astype(BF16)
        if s in (1, 2, 3):
            send_b[8 - s] = (ce - co + se - so).astype(BF16)

    copies_b = [
        remote(send_b.at[lax.rem(me_s + k, SEQ_DEV)], recv_b.at[me_s], sem_b, k, on_seq(k))
        for k in SEQ_ORDER
    ]
    recv_b[me_s] = send_b[me_s]
    finish(copies_v)
    for o in range(2):
        total = recv_v[o, 0].astype(F32)
        for n in range(1, NEAR):
            total = total + recv_v[o, n].astype(F32)
        v_near[me_s, o] = total.astype(BF16)
    copies_u = [
        remote(v_near.at[me_s], v_near.at[me_s], sem_u, k, on_seq(k)) for k in SEQ_ORDER
    ]
    finish(copies_w)
    copies_k = [
        remote(w_group.at[o, half], w_group.at[o, half], sem_k, o, other_core) for o in range(2)
    ]
    finish(in_gate, copies_b)
    own = [pl.ds(pl.multiple_of(member[o] * CHANS, CHANS), CHANS) for o in range(2)]
    others = [
        pl.ds(pl.multiple_of((member[o] + 1 - 2 * beside) * CHANS, CHANS), CHANS) for o in range(2)
    ]
    convolved = block_transpose([recv_b[d].astype(F32) for d in range(8)])
    copies_g, copies_m = [], []
    for i in range(CHUNKS):
        for q in range(i * 8 // CHUNKS, (i + 1) * 8 // CHUNKS):
            rows = slice(q * SUB, (q + 1) * SUB)
            value = convolved[q] + skip[...] * sig[rows, :].astype(F32)
            depth[rows, own[i % 2]] = (gat[rows, :].astype(F32) * value).astype(BF16)
        o, at = i % 2, i * NEAR
        block = depth.at[i * STEP : (i + 1) * STEP, own[o]]
        copies_m.append(remote(block, block, sem_g, at, other_line))
        copies_g.append([remote(block, block, sem_g, at + k, on_line(o, k)) for k in range(1, FAR)])
    for i in range(CHUNKS):
        o, at = i % 2, i * NEAR + FAR
        copies_m[i].wait_recv()
        block = depth.at[i * STEP : (i + 1) * STEP, others[o]]
        copies_g[i] += [remote(block, block, sem_g, at + k, on_line(o, k)) for k in range(1, FAR)]

    copies_p, copies_q, copies_y = [], [], []

    def sum_y(i):
        finish(copies_q[i])
        total = part_y[i, 0].astype(F32)
        for f in range(1, FAR):
            total = total + part_y[i, f].astype(F32)
        o = i % 2
        near_y[i, member[o]] = total.astype(BF16)
        block = near_y.at[i, member[o]]
        copies_y.append(
            [remote(block, block, sem_y, i * NEAR + k, on_member(o, k)) for k in range(1, NEAR)]
        )

    finish(copies_k, copies_u)
    for i in range(CHUNKS):
        rows, o = slice(i * STEP, (i + 1) * STEP), i % 2
        finish(copies_g[i])
        block = depth[rows, :]
        product = jnp.concatenate([v_near[s, o] for s in range(SEQ_DEV)], 1)
        part_y[i, group[o]] = lax.dot_general(
            product, block, (((1,), (1,)), ((), ())), preferred_element_type=F32
        ).astype(BF16)
        sums = part_y.at[i, group[o]]
        copies_q.append([remote(sums, sums, sem_q, i * FAR + k, on_far(o, k)) for k in range(1, FAR)])
    for i in range(CHUNKS):
        rows, o = slice(i * STEP, (i + 1) * STEP), i % 2
        projected = dot(depth[rows, :], w_group[o].reshape(NEAR * CHANS, FAR * CHANS))
        for f in range(FAR):
            part[f, rows, :] = projected[:, f * CHANS : (f + 1) * CHANS].astype(BF16)
        copies_p.append(
            [
                remote(
                    part.at[lax.rem(group[o] + k, FAR), rows, :], recv_p.at[group[o], rows, :],
                    sem_p, i * FAR + k, on_far(o, k),
                )
                for k in range(1, FAR)
            ]
        )
        recv_p[group[o], rows, :] = part[group[o], rows, :]
    for i in range(CHUNKS):
        sum_y(i)
    for i in range(CHUNKS):
        rows = slice(i * STEP, (i + 1) * STEP)
        finish(copies_p[i])
        total = recv_p[0, rows, :].astype(F32)
        for f in range(1, FAR):
            total = total + recv_p[f, rows, :].astype(F32)
        mixed[rows, :] = total.astype(BF16)
    stores = [local(14, mixed, to_mixed)]

    sum_z = jnp.zeros((RANK, CHANS), F32)
    for i in range(CHUNKS):
        finish(copies_y[i])
        sum_z = sum_z + dot(near_y[i].reshape(RANK, STEP), mixed[i * STEP : (i + 1) * STEP, :])
    part_z[...] = (sum_z * np.float32(1.0 / (SEQ_DEV * ROWS))).reshape(2, CHANS, CHANS)
    send_z[...] = part_z[1 - core].astype(BF16)
    copies_c = [remote(send_z, recv_z, sem_c, 0, other_core)]
    finish(copies_c)
    high = me_s // 2
    recv_h[high] = (part_z[core] + recv_z[...].astype(F32)).astype(BF16)
    copies_h = [remote(recv_h.at[high], recv_h.at[high], sem_h, k, on_seq(2 * k)) for k in (2, 1, 3)]
    for i in range(CHUNKS):
        out_y[i * STEP : (i + 1) * STEP, :] = near_y[i].reshape(RANK, STEP).astype(F32).T
    stores.append(local(15, out_y, to_y))
    settle()
    finish(copies_h)
    total = recv_h[0].astype(F32)
    for h in range(1, 4):
        total = total + recv_h[h].astype(F32)
    full_z[core] = total.astype(BF16)
    copies_f = [remote(full_z.at[core], full_z.at[core], sem_f, 0, other_core)]
    finish(copies_f)
    out_z[...] = full_z[...].reshape(RANK, CHANS).astype(F32).T
    stores.append(local(16, out_z, to_z))
    settle()
    finish(stores)


def store(*refs):
    ins, outs, held, sems = refs[:3], refs[3:6], refs[6:9], refs[9]
    first = [pltpu.make_async_copy(a, b, sems.at[0, k]) for k, (a, b) in enumerate(zip(ins, held))]
    second = [pltpu.make_async_copy(a, b, sems.at[1, k]) for k, (a, b) in enumerate(zip(held, outs))]
    for copy in first:
        copy.start()
    for k in range(3):
        first[k].wait()
        second[k].start()
    for copy in second:
        copy.wait()


def per_device(signal, gating, filter_taps, skip_bias, out_weight, test_matrix):
    constants = [jnp.asarray(t) for t in tables()]
    weight = out_weight.reshape(FAR, FAR, 2 * CHANS, CHANS)
    args = [signal, gating, filter_taps, skip_bias[None, :], weight, test_matrix] + constants
    outs = (
        jax.ShapeDtypeStruct((ROWS, CHANS), BF16),
        jax.ShapeDtypeStruct((ROWS, RANK), F32),
        jax.ShapeDtypeStruct((CHANS, RANK), F32),
    )

    def sems(n):
        return pltpu.SemaphoreType.DMA((2, n))

    results = pl.pallas_call(
        kernel,
        out_shape=outs,
        in_specs=[pl.BlockSpec(memory_space=pl.ANY)] * len(args),
        out_specs=(pl.BlockSpec(memory_space=pl.ANY),) * 3,
        scratch_shapes=[pltpu.VMEM(o.shape, o.dtype) for o in outs]
        + [
            pltpu.VMEM((ROWS, CHANS), BF16),
            pltpu.VMEM((ROWS, CHANS), BF16),
            pltpu.VMEM((ROWS, CHANS), BF16),
            pltpu.VMEM((1, CHANS), F32),
        ]
        + [pltpu.VMEM(c.shape, c.dtype) for c in constants]
        + [
            pltpu.SemaphoreType.DMA((17,)),
            pltpu.VMEM((SEQ_DEV, 2 * SUB, 128), BF16),
            pltpu.VMEM((SEQ_DEV, 2 * SUB, 128), BF16),
            pltpu.VMEM((SEQ_DEV, SUB, 128), BF16),
            pltpu.VMEM((SEQ_DEV, SUB, 128), BF16),
            pltpu.VMEM((ROWS, NEAR * CHANS), BF16),
            pltpu.VMEM((2, FAR, 2 * CHANS, FAR * CHANS), BF16),
            pltpu.VMEM((FAR, ROWS, CHANS), BF16),
            pltpu.VMEM((FAR, ROWS, CHANS), BF16),
            pltpu.VMEM((COARSE, 2 * SUB, 256), F32),
            pltpu.VMEM((COARSE, SUB, 256), F32),
            pltpu.VMEM((2, FAR, CHANS, RANK), BF16),
            pltpu.VMEM((2, CHANS, FAR * CHANS), BF16),
            pltpu.VMEM((2, NEAR, SLICE, CHANS), BF16),
            pltpu.VMEM((2, NEAR, SLICE, CHANS), BF16),
            pltpu.VMEM((SEQ_DEV, 2, SLICE, CHANS), BF16),
            pltpu.VMEM((CHUNKS, FAR, SLICE, STEP), BF16),
            pltpu.VMEM((CHUNKS, NEAR, SLICE, STEP), BF16),
            pltpu.VMEM((2, CHANS, CHANS), F32),
            pltpu.VMEM((CHANS, CHANS), BF16),
            pltpu.VMEM((CHANS, CHANS), BF16),
            pltpu.VMEM((4, CHANS, CHANS), BF16),
            pltpu.VMEM((2, CHANS, CHANS), BF16),
            sems(SEQ_DEV), sems(SEQ_DEV), sems(CHUNKS * NEAR), sems(2 * FAR), sems(2 * FAR),
            sems(2 * FAR), sems(2 * NEAR), sems(SEQ_DEV), sems(CHUNKS * FAR), sems(CHUNKS * FAR), sems(CHUNKS * NEAR),
            sems(1), sems(4), sems(1), sems(2),
        ],
        compiler_params=pltpu.CompilerParams(
            collective_id=0, has_side_effects=True, vmem_limit_bytes=60 * 2**20
        ),
    )(*args)
    return pl.pallas_call(
        store,
        out_shape=outs,
        in_specs=[pl.BlockSpec(memory_space=pl.ANY)] * 3,
        out_specs=(pl.BlockSpec(memory_space=pl.ANY),) * 3,
        scratch_shapes=[pltpu.VMEM(o.shape, o.dtype) for o in outs]
        + [pltpu.SemaphoreType.DMA((2, 3))],
        compiler_params=pltpu.CompilerParams(vmem_limit_bytes=60 * 2**20),
    )(*results)


def solution(mesh):
    return jax.shard_map(
        per_device,
        mesh=mesh,
        in_specs=(
            P("seq", "chan"), P("seq", "chan"), P("seq", "chan"),
            P("chan"), P(None, "chan"), P("chan", None),
        ),
        out_specs=(P("seq", "chan"), P("seq", None), P("chan", None)),
        check_vma=False,
    )
```
